128 devices in a mesh: aux: 16 (over x, z), bas: 8 (over y, core).
Axes of the slice: x: 4, y: 4, z: 4, core: 2. Of those that a mesh axis runs over, the one named last changes fastest.
Arguments:
- integrals: bfloat16 [30720, 384, 128], P('aux', 'bas'), as said below
- coefficients: bfloat16 [128, 64], replicated, may hold values from -0.875 to 0.875
- supports: int32 [64, 3], replicated, may hold values from 0 to 7, all different within a row
- tile_pattern: int32 [240, 24], P('aux', 'bas'), may hold values 0 or 1
Outputs:
- exchange_matrix: float32 [384, 384], P(('aux', 'bas'))
The draws below stay inside these ranges and needn't reach their ends.
Inputs may be any that keep to these rules, and one draw needn't show every extreme that they name: `supports`: each row names 3 different tiles. `integrals`: entries lie within 8 / sqrt(1966080) of zero.
All inputs are finite; a program needn't handle non-finite values. No bound on the sum of `tile_pattern` on one device may be relied on, other than what follows from the above.
Results may differ from the reference program's by a relative error of at most 0.0003.
Values may be sent and summed in bfloat16 or wider, within the bound.
A program may use at most 192 MiB of HBM per device.

```python
import jax
import jax.numpy as jnp
from jax import lax

AUX_TOTAL = 30720
AUX_TILE = 128
BAS_TILE = 16
ORB_SPAN = 128
ORBITALS = 64
SUPPORT = 3
WINDOW = 384


def draw_integrals(key, part):
    first_key, second_key = jax.random.split(jax.random.fold_in(key, 11))
    scale = (AUX_TOTAL * ORBITALS) ** (-0.5)
    own_part = jnp.clip(jax.random.normal(first_key, (AUX_TOTAL, WINDOW, ORB_SPAN), jnp.float32), -4.0, 4.0)
    shared = jnp.clip(jax.random.normal(second_key, (AUX_TOTAL, WINDOW // BAS_TILE, 1, ORB_SPAN), jnp.float32), -4.0, 4.0)
    shared = jnp.broadcast_to(shared, (AUX_TOTAL, WINDOW // BAS_TILE, BAS_TILE, ORB_SPAN)).reshape(AUX_TOTAL, WINDOW, ORB_SPAN)
    return ((own_part + shared) * scale).astype(jnp.bfloat16)


def with_ends(array, stream_key, low, top_value):
    extent = array.shape
    place = [jax.random.randint(jax.random.fold_in(stream_key, axis), (), 0, extent[axis]) for axis in range(len(extent))]
    array = array.at[tuple(place)].set(low)
    longest = extent.index(max(extent))
    place[longest] = (place[longest] + 1) % extent[longest]
    return array.at[tuple(place)].set(top_value)


def distinct(key, rows, number_of, top, lift):
    ranking = jax.random.permutation(jax.random.fold_in(key, 1), number_of)
    boost = ranking
    for power in range(3):
        boost = boost * boost // number_of
    boost = boost * lift // number_of
    lots = jax.random.randint(jax.random.fold_in(key, 2), (rows, number_of), 0, 4096) + boost
    holders = jax.random.permutation(jax.random.fold_in(key, 3), rows)[jnp.arange(number_of) % rows]
    lots = jnp.where(jnp.arange(rows)[:, None] == holders[None, :], 1 << 14, lots)
    score = lots * number_of + jnp.arange(number_of)
    return lax.top_k(score.astype(jnp.int32), top)[1].astype(jnp.int32)


def bell_draw(own_key, dims, deviation, bound, kind=jnp.bfloat16):
    array = jax.random.normal(own_key, dims, jnp.float32) * deviation
    return jnp.minimum(jnp.maximum(array, -bound), bound).astype(kind)


def setup_inputs(seed: int = 0) -> dict:
    splits = jax.random.split(jax.random.key(seed), 5)
    integrals = draw_integrals(jax.random.fold_in(splits[4], 71), 0)
    coefficients = bell_draw(splits[1], (ORB_SPAN, ORBITALS), (SUPPORT * BAS_TILE) ** -0.5, 0.875)
    supports = distinct(splits[2], ORBITALS, ORB_SPAN // BAS_TILE, SUPPORT, 0)
    tile_pattern = with_ends((jax.random.randint(splits[3], (AUX_TOTAL // AUX_TILE, WINDOW // BAS_TILE), 0, 2) < 1).astype(jnp.int32), jax.random.fold_in(splits[3], 1), 0, 1)
    return {"integrals": integrals, "coefficients": coefficients, "supports": supports, "tile_pattern": tile_pattern}


def reference(integrals, coefficients, supports, tile_pattern):
    tile_of = jnp.arange(ORB_SPAN) // BAS_TILE
    supported = jnp.any(tile_of[:, None, None] == supports[None, :, :], axis=2)
    orbitals = jnp.where(supported, coefficients, jnp.zeros_like(coefficients))
    orbital_wide = orbitals.astype(jnp.float32)
    screening = jnp.repeat(tile_pattern, BAS_TILE, axis=1).astype(jnp.float32)
    aux_blocks = integrals.reshape(AUX_TOTAL // AUX_TILE, AUX_TILE, WINDOW, ORB_SPAN)

    def accumulate(summed, pieces):
        aux_block, screen_row = pieces
        transformed = jnp.einsum('pmn,ni->pim', aux_block.astype(jnp.float32), orbital_wide)
        transformed = (transformed * screen_row[None, None, :]).astype(jnp.bfloat16)
        stacked = transformed.reshape(AUX_TILE * ORBITALS, WINDOW)
        return summed + jnp.dot(stacked.T, stacked, preferred_element_type=jnp.float32), None

    initial = jnp.zeros((WINDOW, WINDOW), jnp.float32)
    summed, unused = lax.scan(accumulate, initial, (aux_blocks, screening))
    return summed
```

```python
import functools

import jax
import jax.numpy as jnp
from jax import lax
from jax.experimental import pallas as pl
from jax.experimental.pallas import tpu as pltpu
from jax.sharding import PartitionSpec as P

AUX_TILE = 128
BAS_TILE = 16
ORBITALS = 64
SPAN = 128
MESH = pl.DeviceIdType.MESH

CAP = 31
SPARE = 8
STAGES = (1, 2, 4, 4, 4, 4, 4, 4, 4)
HANDOVER_AFTER = 2


def dense_body(integrals, coefficients, supports, tile_pattern):
    span = integrals.shape[2]
    tile_of = jnp.arange(span) // BAS_TILE
    supported = jnp.any(tile_of[:, None, None] == supports[None, :, :], axis=2)
    orbitals = jnp.where(supported, coefficients, jnp.zeros_like(coefficients))
    screening = jnp.repeat(jnp.repeat(tile_pattern, BAS_TILE, axis=1), AUX_TILE, axis=0).astype(
        jnp.float32
    )
    transformed = jnp.einsum("pmn,ni->pim", integrals, orbitals, preferred_element_type=jnp.float32)
    transformed = (transformed * screening[:, None, :]).astype(jnp.bfloat16)
    contract = (((0,), (0,)), ((), ()))
    redistributed = lax.all_to_all(transformed, "bas", split_axis=1, concat_axis=2, tiled=True)
    window_rows = redistributed.shape[2]
    stacked = redistributed.reshape(-1, window_rows)
    return lax.psum_scatter(
        lax.dot_general(stacked, stacked, contract, preferred_element_type=jnp.float32),
        ("aux", "bas"),
        scatter_dimension=0,
        tiled=True,
    )


def kernel(
    n_aux,
    n_bas,
    tiles,
    blocks,
    pattern_smem,
    pattern_vmem,
    supports_ref,
    coefficients_ref,
    integrals_ref,
    out_ref,
    flag_ref,
    loaded,
    weights,
    send_buf,
    recv_buf,
    spare_out,
    spare_in,
    dense,
    partial,
    partial_in,
    summed,
    summed_in,
    pattern_out,
    pattern_in,
    pattern_all,
    following,
    listed,
    load_sem,
    pattern_send,
    pattern_recv,
    pattern_local,
    send_sem,
    recv_sem,
    own_sem,
    spare_send,
    spare_recv,
    aux_send,
    aux_recv,
    bas_send,
    bas_recv,
):
    my_aux = lax.axis_index("aux")
    me = lax.axis_index("bas")
    sibling = me + 1 - 2 * lax.rem(me, 2)
    count = tiles * blocks
    rows = AUX_TILE // n_bas // 2 * BAS_TILE

    loads = []
    for q in range(tiles):
        loads.append(
            pltpu.make_async_copy(integrals_ref.at[q], loaded.at[q], load_sem.at[q])
        )
        loads[-1].start()

    barrier = pltpu.get_barrier_semaphore()
    for k in range(1, n_bas):
        pl.semaphore_signal(
            barrier, inc=1, device_id={"bas": lax.rem(me + k, n_bas)}, device_id_type=MESH
        )
    for k in range(1, n_aux):
        pl.semaphore_signal(
            barrier, inc=1, device_id={"aux": lax.rem(my_aux + k, n_aux)}, device_id_type=MESH
        )

    following[count] = jnp.int32(count - 1)
    upcoming = jnp.int32(count - 1)
    for at in reversed(range(count)):
        upcoming = jnp.where(pattern_smem[at % blocks, at // blocks] > 0, at, upcoming)
        following[at] = upcoming
    at = following[0]
    for s in range(CAP + SPARE):
        listed[s] = at
        at = following[at + 1]
    mine = jnp.int32(0)
    for at in range(count):
        mine = mine + pattern_smem[at % blocks, at // blocks]

    pattern_out[...] = jnp.zeros_like(pattern_out)
    pattern_out[0:blocks, 0:tiles] = pattern_vmem[...]

    tile_of = lax.broadcasted_iota(jnp.int32, (ORBITALS, SPAN), 1) // BAS_TILE
    named = supports_ref[...]
    supported = (
        (tile_of == named[:, 0:1]) | (tile_of == named[:, 1:2]) | (tile_of == named[:, 2:3])
    )
    orbitals = jnp.where(supported, coefficients_ref[...].astype(jnp.float32), 0.0)
    weights[...] = jnp.zeros_like(weights)
    weights[0:ORBITALS, 0:SPAN] = orbitals.astype(jnp.bfloat16)
    weights[ORBITALS : 2 * ORBITALS, SPAN : 2 * SPAN] = orbitals.astype(jnp.bfloat16)

    pl.semaphore_wait(barrier, n_bas + n_aux - 2)

    pattern_copies = []
    for k in range(1, n_bas):
        pattern_copies.append(
            pltpu.make_async_remote_copy(
                src_ref=pattern_out,
                dst_ref=pattern_in.at[me],
                send_sem=pattern_send.at[k],
                recv_sem=pattern_recv.at[k],
                device_id={"bas": lax.rem(me + k, n_bas)},
                device_id_type=MESH,
            )
        )
        pattern_copies[-1].start()

    for copy in loads:
        copy.wait()

    def transform(s, share):
        at = listed[s]
        tile = at // blocks
        block = at - tile * blocks
        width = AUX_TILE // n_bas
        part = loaded[tile, pl.ds(share * width, width), block]
        part = part.reshape(width // 2, 2, BAS_TILE, SPAN)
        left = jnp.concatenate(
            [part[:, 0].reshape(rows, SPAN), part[:, 1].reshape(rows, SPAN)], axis=1
        )
        return lax.dot_general(
            left, weights[...], (((1,), (1,)), ((), ())), preferred_element_type=jnp.float32
        ).astype(jnp.bfloat16)

    copies = []
    hand = None
    first = 0
    for stage, size in enumerate(STAGES):
        if first + size > CAP - SPARE and hand is not None:
            hand.wait()
            hand = None

        def fill(s, carry, mixed=first + size > CAP - SPARE):
            for share in range(n_bas):
                value = transform(s, share)
                if mixed:
                    other = spare_in[CAP - 1 - s, share]
                    value = jnp.where(s < mine, value, other)
                send_buf[share, s] = value
            return carry

        lax.fori_loop(first, first + size, fill, 0)
        for k in range(1, n_bas):
            peer = lax.rem(me + k, n_bas)
            copies.append(
                pltpu.make_async_remote_copy(
                    src_ref=send_buf.at[peer, pl.ds(first, size)],
                    dst_ref=recv_buf.at[me, pl.ds(first, size)],
                    send_sem=send_sem.at[stage, k],
                    recv_sem=recv_sem.at[stage, k],
                    device_id={"bas": peer},
                    device_id_type=MESH,
                )
            )
            copies[-1].start()
        if stage == HANDOVER_AFTER:

            def spare(e, carry):
                for share in range(n_bas):
                    spare_out[e, share] = transform(CAP + e, share)
                return carry

            lax.fori_loop(0, SPARE, spare, 0)
            hand = pltpu.make_async_remote_copy(
                src_ref=spare_out,
                dst_ref=spare_in,
                send_sem=spare_send,
                recv_sem=spare_recv,
                device_id={"bas": sibling},
                device_id_type=MESH,
            )
            hand.start()
        first += size
    own = pltpu.make_async_copy(send_buf.at[me], recv_buf.at[me, pl.ds(0, CAP)], own_sem)
    own.start()

    recv_buf[0, CAP] = jnp.zeros(recv_buf.shape[2:], recv_buf.dtype)
    for copy in pattern_copies:
        copy.wait()
    pattern_in[me] = pattern_out[...]
    local = pltpu.make_async_copy(pattern_in, pattern_all, pattern_local)
    local.start()
    local.wait()

    def tally(q, counts):
        return tuple(
            counts[d] + sum(pattern_all[d, b, q] for b in range(blocks)) for d in range(n_bas)
        )

    counts = lax.fori_loop(0, tiles, tally, (jnp.int32(0),) * n_bas)
    over = jnp.int32(0)
    for d in range(0, n_bas, 2):
        over = jnp.where(counts[d] + counts[d + 1] > 2 * CAP, 1, over)
    for d in range(n_bas):
        over = jnp.where(counts[d] > CAP + SPARE, 1, over)

    own.wait()
    for copy in copies:
        copy.wait()

    span_rows = n_bas * blocks * BAS_TILE
    aux_rows = span_rows // n_aux
    for a in range(n_aux):
        partial[a, 0:aux_rows] = jnp.zeros((aux_rows, span_rows), jnp.float32)
        partial[a, aux_rows:] = jnp.full(
            (partial.shape[1] - aux_rows, span_rows), over, jnp.int32
        ).astype(jnp.float32)

    def gram(q, ranks):
        ranks = list(ranks)
        for d in range(n_bas):
            for b in range(blocks):
                here = pattern_all[d, b, q]
                rank = ranks[d]
                handed = rank >= CAP
                source = jnp.where(handed, d + 1 - 2 * (d % 2), d)
                slot = jnp.where(handed, jnp.maximum(2 * CAP - 1 - rank, 0), rank)
                source = jnp.where(here > 0, source, 0)
                slot = jnp.where(here > 0, slot, CAP)
                value = recv_buf[source, slot]
                top = (d * blocks + b) * BAS_TILE
                for u in range(rows // BAS_TILE):
                    dense[top : top + BAS_TILE, u * 128 : (u + 1) * 128] = value[
                        u * BAS_TILE : (u + 1) * BAS_TILE
                    ]
                ranks[d] = rank + here
        product = lax.dot_general(
            dense[...], dense[...], (((1,), (1,)), ((), ())), preferred_element_type=jnp.float32
        )
        for a in range(n_aux):
            partial[a, 0:aux_rows] += product[a * aux_rows : (a + 1) * aux_rows]
        return tuple(ranks)

    lax.fori_loop(0, tiles, gram, (jnp.int32(0),) * n_bas)

    copies = []
    for k in range(1, n_aux):
        peer = lax.rem(my_aux + k, n_aux)
        copies.append(
            pltpu.make_async_remote_copy(
                src_ref=partial.at[peer],
                dst_ref=partial_in.at[my_aux],
                send_sem=aux_send.at[k],
                recv_sem=aux_recv.at[k],
                device_id={"aux": peer},
                device_id_type=MESH,
            )
        )
        copies[-1].start()
    partial_in[my_aux] = partial[my_aux]
    for copy in copies:
        copy.wait()
    total = partial_in[0]
    for a in range(1, n_aux):
        total = total + partial_in[a]
    flag_ref[...] = total[aux_rows:, 0:128]

    own_rows = aux_rows // n_bas
    for d in range(n_bas):
        summed[d, 0:own_rows] = total[d * own_rows : (d + 1) * own_rows]
    copies = []
    for k in range(1, n_bas):
        peer = lax.rem(me + k, n_bas)
        copies.append(
            pltpu.make_async_remote_copy(
                src_ref=summed.at[peer],
                dst_ref=summed_in.at[me],
                send_sem=bas_send.at[k],
                recv_sem=bas_recv.at[k],
                device_id={"bas": peer},
                device_id_type=MESH,
            )
        )
        copies[-1].start()
    summed_in[me] = summed[me]
    for copy in copies:
        copy.wait()
    total = summed_in[0]
    for d in range(1, n_bas):
        total = total + summed_in[d]
    out_ref[...] = total[0:own_rows]


def body(n_aux, n_bas, integrals, coefficients, supports, tile_pattern):
    tiles, blocks = tile_pattern.shape
    window = n_bas * blocks * BAS_TILE
    rows = AUX_TILE // n_bas // 2 * BAS_TILE
    aux_rows = window // n_aux
    own_rows = aux_rows // n_bas
    vmem = pl.BlockSpec(memory_space=pltpu.VMEM)
    dma = pltpu.SemaphoreType.DMA
    bf16, f32, i32 = jnp.bfloat16, jnp.float32, jnp.int32
    result, flag = pl.pallas_call(
        functools.partial(kernel, n_aux, n_bas, tiles, blocks),
        out_shape=(
            jax.ShapeDtypeStruct((own_rows, window), f32),
            jax.ShapeDtypeStruct((8, 128), f32),
        ),
        in_specs=[
            pl.BlockSpec(memory_space=pltpu.SMEM),
            vmem,
            vmem,
            vmem,
            pl.BlockSpec(memory_space=pl.ANY),
        ],
        out_specs=(vmem, vmem),
        scratch_shapes=[
            pltpu.VMEM((tiles, AUX_TILE, blocks, BAS_TILE, SPAN), bf16),
            pltpu.VMEM((2 * ORBITALS, 2 * SPAN), bf16),
            pltpu.VMEM((n_bas, CAP, rows, 2 * ORBITALS), bf16),
            pltpu.VMEM((n_bas, CAP + 1, rows, 2 * ORBITALS), bf16),
            pltpu.VMEM((SPARE, n_bas, rows, 2 * ORBITALS), bf16),
            pltpu.VMEM((SPARE, n_bas, rows, 2 * ORBITALS), bf16),
            pltpu.VMEM((window, rows // BAS_TILE * 2 * ORBITALS), bf16),
            pltpu.VMEM((n_aux, aux_rows + 8, window), f32),
            pltpu.VMEM((n_aux, aux_rows + 8, window), f32),
            pltpu.VMEM((n_bas, 8, window), f32),
            pltpu.VMEM((n_bas, 8, window), f32),
            pltpu.VMEM((8, 128), i32),
            pltpu.VMEM((n_bas, 8, 128), i32),
            pltpu.SMEM((n_bas, 8, 128), i32),
            pltpu.SMEM((tiles * blocks + 1,), i32),
            pltpu.SMEM((CAP + SPARE,), i32),
            dma((tiles,)),
            dma((n_bas,)),
            dma((n_bas,)),
            dma,
            dma((len(STAGES), n_bas)),
            dma((len(STAGES), n_bas)),
            dma,
            dma,
            dma,
            dma((n_aux,)),
            dma((n_aux,)),
            dma((n_bas,)),
            dma((n_bas,)),
        ],
        compiler_params=pltpu.CompilerParams(
            collective_id=0, has_side_effects=True, vmem_limit_bytes=60 * 2**20
        ),
        name="exchange",
    )(
        tile_pattern.T,
        tile_pattern.T,
        supports,
        coefficients.T,
        integrals.reshape(tiles, AUX_TILE, blocks, BAS_TILE, SPAN),
    )
    return lax.cond(
        flag[0, 0] > 0.0,
        lambda: dense_body(integrals, coefficients, supports, tile_pattern),
        lambda: result,
    )


def solution(mesh):
    in_specs = (P("aux", "bas", None), P(), P(), P("aux", "bas"))
    out_specs = P(("aux", "bas"), None)
    return jax.shard_map(
        functools.partial(body, mesh.shape["aux"], mesh.shape["bas"]),
        mesh=mesh,
        in_specs=in_specs,
        out_specs=out_specs,
        check_vma=False,
    )
```

```python
import functools

import jax
import jax.numpy as jnp
from jax import lax
from jax.experimental import pallas as pl
from jax.experimental.pallas import tpu as pltpu
from jax.sharding import PartitionSpec as P

AUX_TILE = 128
BAS_TILE = 16
ORBITALS = 64
SPAN = 128
MESH = pl.DeviceIdType.MESH

CAP = 31
SPARE = 8
STAGES = (3, 4, 4, 4, 4, 4, 4, 4)
HANDOVER_AFTER = 1
HEAD = 3
HEAD_TILES = 4
EARLY_TILES = 9
EARLY = 27
GROUP = 3


def dense_body(integrals, coefficients, supports, tile_pattern):
    span = integrals.shape[2]
    tile_of = jnp.arange(span) // BAS_TILE
    supported = jnp.any(tile_of[:, None, None] == supports[None, :, :], axis=2)
    orbitals = jnp.where(supported, coefficients, jnp.zeros_like(coefficients))
    screening = jnp.repeat(jnp.repeat(tile_pattern, BAS_TILE, axis=1), AUX_TILE, axis=0).astype(
        jnp.float32
    )
    transformed = jnp.einsum("pmn,ni->pim", integrals, orbitals, preferred_element_type=jnp.float32)
    transformed = (transformed * screening[:, None, :]).astype(jnp.bfloat16)
    contract = (((0,), (0,)), ((), ()))
    redistributed = lax.all_to_all(transformed, "bas", split_axis=1, concat_axis=2, tiled=True)
    window_rows = redistributed.shape[2]
    stacked = redistributed.reshape(-1, window_rows)
    total = lax.dot_general(stacked, stacked, contract, preferred_element_type=jnp.float32)
    for axis in ("aux", "bas"):
        total = total.reshape(lax.axis_size(axis), -1, window_rows)
        total = jnp.sum(lax.all_to_all(total, axis, split_axis=0, concat_axis=0), axis=0)
    return total


def kernel(
    n_aux,
    n_bas,
    tiles,
    blocks,
    pattern_smem,
    pattern_vmem,
    supports_ref,
    coefficients_ref,
    integrals_ref,
    out_ref,
    flag_ref,
    loaded_head,
    loaded,
    weights,
    send_buf,
    recv_early,
    recv_late,
    spare_out,
    spare_in,
    dense,
    wide,
    corner,
    partial,
    pair_in,
    half,
    partial_in,
    summed,
    summed_in,
    pattern_out,
    pattern_in,
    pattern_all,
    flag_out,
    flag_in,
    flag_smem,
    following,
    listed,
    head_sem,
    load_sem,
    pattern_send,
    pattern_recv,
    pattern_local,
    send_sem,
    recv_sem,
    own_sem,
    spare_send,
    spare_recv,
    flag_send,
    flag_recv,
    flag_local,
    pair_send,
    pair_recv,
    aux_send,
    aux_recv,
    bas_send,
    bas_recv,
):
    my_aux = lax.axis_index("aux")
    me = lax.axis_index("bas")
    sibling = me + 1 - 2 * lax.rem(me, 2)
    count = tiles * blocks
    rows = AUX_TILE // n_bas // 2 * BAS_TILE

    head = pltpu.make_async_copy(integrals_ref.at[pl.ds(0, HEAD_TILES)], loaded_head, head_sem)
    head.start()
    loads = []
    for q in range(HEAD_TILES, tiles):
        loads.append(
            pltpu.make_async_copy(integrals_ref.at[q], loaded.at[q], load_sem.at[q])
        )
        loads[-1].start()

    barrier = pltpu.get_barrier_semaphore()
    for k in range(1, n_bas):
        pl.semaphore_signal(
            barrier, inc=1, device_id={"bas": lax.rem(me + k, n_bas)}, device_id_type=MESH
        )
    for k in range(1, n_aux):
        pl.semaphore_signal(
            barrier, inc=1, device_id={"aux": lax.rem(my_aux + k, n_aux)}, device_id_type=MESH
        )

    following[count] = jnp.int32(count - 1)
    upcoming = jnp.int32(count - 1)
    for at in reversed(range(count)):
        upcoming = jnp.where(pattern_smem[at % blocks, at // blocks] > 0, at, upcoming)
        following[at] = upcoming
    mine = jnp.int32(0)
    for at in range(count):
        if at == HEAD_TILES * blocks:
            short = mine < HEAD
            mine = jnp.maximum(mine, HEAD)
        mine = mine + pattern_smem[at % blocks, at // blocks]
    at = following[0]
    for s in range(CAP + SPARE):
        if s == HEAD:
            at = jnp.where(short, following[HEAD_TILES * blocks], at)
        listed[s] = at
        at = following[at + 1]

    pattern_out[...] = jnp.zeros_like(pattern_out)
    pattern_out[0:blocks, 0:tiles] = pattern_vmem[...]

    tile_of = lax.broadcasted_iota(jnp.int32, (SPAN, ORBITALS), 0) // BAS_TILE
    named = supports_ref[...]
    supported = tile_of == named[0:1]
    for k in range(1, named.shape[0]):
        supported = supported | (tile_of == named[k : k + 1])
    diagonal = lax.broadcasted_iota(jnp.int32, (ORBITALS, ORBITALS), 0) == (
        lax.broadcasted_iota(jnp.int32, (ORBITALS, ORBITALS), 1)
    )
    turned = lax.dot_general(
        jnp.where(diagonal, 1.0, 0.0).astype(jnp.bfloat16),
        jnp.where(supported, 1.0, 0.0).astype(jnp.bfloat16),
        (((1,), (1,)), ((), ())),
        preferred_element_type=jnp.float32,
    )
    orbitals = jnp.where(turned > 0.5, coefficients_ref[...].astype(jnp.float32), 0.0)
    weights[...] = jnp.zeros_like(weights)
    weights[0:ORBITALS, 0:SPAN] = orbitals.astype(jnp.bfloat16)
    weights[ORBITALS : 2 * ORBITALS, SPAN : 2 * SPAN] = orbitals.astype(jnp.bfloat16)

    head.wait()
    loads.append(pltpu.make_async_copy(loaded_head, loaded.at[pl.ds(0, HEAD_TILES)], head_sem))
    loads[-1].start()

    def transform(s, share, source, limit):
        at = jnp.minimum(listed[s], limit * blocks - 1)
        tile = at // blocks
        block = at - tile * blocks
        width = AUX_TILE // n_bas
        part = source[tile, pl.ds(share * width, width), block]
        part = part.reshape(width // 2, 2, BAS_TILE, SPAN)
        left = jnp.concatenate(
            [part[:, 0].reshape(rows, SPAN), part[:, 1].reshape(rows, SPAN)], axis=1
        )
        return lax.dot_general(
            left, weights[...], (((1,), (1,)), ((), ())), preferred_element_type=jnp.float32
        ).astype(jnp.bfloat16)

    copies = []
    hand = None
    first = 0
    for stage, size in enumerate(STAGES):
        if first + size > CAP - SPARE and hand is not None:
            hand.wait()
            hand = None

        if first == HEAD:
            for copy in loads:
                copy.wait()
        source, limit = (loaded_head, HEAD_TILES) if first < HEAD else (loaded, tiles)

        def fill(s, carry, mixed=first + size > CAP - SPARE, source=source, limit=limit):
            for share in range(n_bas):
                value = transform(s, share, source, limit)
                if mixed:
                    other = spare_in[CAP - 1 - s, share]
                    value = jnp.where(s < mine, value, other)
                send_buf[share, s] = value
            return carry

        lax.fori_loop(first, first + size, fill, 0)
        if stage == 0:
            pl.semaphore_wait(barrier, n_bas + n_aux - 2)

            pattern_copies = []
            for k in range(1, n_bas):
                pattern_copies.append(
                    pltpu.make_async_remote_copy(
                        src_ref=pattern_out,
                        dst_ref=pattern_in.at[me],
                        send_sem=pattern_send.at[k],
                        recv_sem=pattern_recv.at[k],
                        device_id={"bas": lax.rem(me + k, n_bas)},
                        device_id_type=MESH,
                    )
                )
                pattern_copies[-1].start()
        for k in range(1, n_bas):
            peer = lax.rem(me + k, n_bas)
            where = (recv_early, first) if first < EARLY else (recv_late, first - EARLY)
            copies.append(
                pltpu.make_async_remote_copy(
                    src_ref=send_buf.at[peer, pl.ds(first, size)],
                    dst_ref=where[0].at[me, pl.ds(where[1], size)],
                    send_sem=send_sem.at[stage, k],
                    recv_sem=recv_sem.at[stage, k],
                    device_id={"bas": peer},
                    device_id_type=MESH,
                )
            )
            copies[-1].start()
        if stage == HANDOVER_AFTER:

            def spare(e, carry):
                for share in range(n_bas):
                    spare_out[e, share] = transform(CAP + e, share, loaded, tiles)
                return carry

            lax.fori_loop(0, SPARE, spare, 0)
            hand = pltpu.make_async_remote_copy(
                src_ref=spare_out,
                dst_ref=spare_in,
                send_sem=spare_send,
                recv_sem=spare_recv,
                device_id={"bas": sibling},
                device_id_type=MESH,
            )
            hand.start()
        first += size
    owns = [
        pltpu.make_async_copy(
            send_buf.at[me, pl.ds(0, EARLY)], recv_early.at[me, pl.ds(0, EARLY)], own_sem.at[0]
        ),
        pltpu.make_async_copy(
            send_buf.at[me, pl.ds(EARLY, CAP - EARLY)],
            recv_late.at[me, pl.ds(0, CAP - EARLY)],
            own_sem.at[1],
        ),
    ]
    for copy in owns:
        copy.start()

    recv_early[0, EARLY] = jnp.zeros(recv_early.shape[2:], recv_early.dtype)
    for copy in pattern_copies:
        copy.wait()
    pattern_in[me] = pattern_out[...]
    local = pltpu.make_async_copy(pattern_in, pattern_all, pattern_local)
    local.start()
    local.wait()

    def tally(q, counts):
        return tuple(
            jnp.where(q == HEAD_TILES, jnp.maximum(counts[d], HEAD), counts[d])
            + sum(pattern_all[d, b, q] for b in range(blocks))
            for d in range(n_bas)
        )

    counts = lax.fori_loop(0, tiles, tally, (jnp.int32(0),) * n_bas)
    over = jnp.int32(0)
    for d in range(0, n_bas, 2):
        over = jnp.where(counts[d] + counts[d + 1] > 2 * CAP, 1, over)
    for d in range(n_bas):
        over = jnp.where(counts[d] > CAP + SPARE, 1, over)
    flag_out[...] = jnp.full(flag_out.shape, over, jnp.int32)
    flag_copies = []
    for k in range(1, n_aux):
        flag_copies.append(
            pltpu.make_async_remote_copy(
                src_ref=flag_out,
                dst_ref=flag_in.at[my_aux],
                send_sem=flag_send.at[k],
                recv_sem=flag_recv.at[k],
                device_id={"aux": lax.rem(my_aux + k, n_aux)},
                device_id_type=MESH,
            )
        )
        flag_copies[-1].start()
    flag_in[my_aux] = flag_out[...]

    span_rows = n_bas * blocks * BAS_TILE
    aux_rows = span_rows // n_aux
    square = wide.shape[1]
    depth = rows // BAS_TILE * 128
    wide[...] = jnp.zeros_like(wide)
    corner[...] = jnp.zeros_like(corner)

    def gram(group, ranks, late):
        ranks = list(ranks)
        for step in range(GROUP):
            q = group * GROUP + step
            for d in range(n_bas):
                ranks[d] = jnp.where(q == HEAD_TILES, jnp.maximum(ranks[d], HEAD), ranks[d])
                for b in range(blocks):
                    here = pattern_all[d, b, q] > 0
                    rank = ranks[d]
                    if late:
                        handed = rank >= CAP
                        source = jnp.where(handed, d + 1 - 2 * (d % 2), d)
                        slot = jnp.where(handed, jnp.maximum(2 * CAP - 1 - rank, 0), rank)
                        last = here & (slot >= EARLY)
                        first = here & (slot < EARLY)
                        value = jnp.where(
                            last,
                            recv_late[source, jnp.clip(slot - EARLY, 0, CAP - EARLY - 1)],
                            recv_early[jnp.where(first, source, 0), jnp.where(first, slot, EARLY)],
                        )
                    else:
                        value = recv_early[jnp.where(here, d, 0), jnp.where(here, rank, EARLY)]
                    top = (d * blocks + b) * BAS_TILE
                    for u in range(rows // BAS_TILE):
                        at = step * depth + u * 128
                        dense[top : top + BAS_TILE, at : at + 128] = value[
                            u * BAS_TILE : (u + 1) * BAS_TILE
                        ]
                    ranks[d] = rank + pattern_all[d, b, q]
        contract = (((1,), (1,)), ((), ()))
        wide[...] += lax.dot_general(
            dense[...], dense[0:square], contract, preferred_element_type=jnp.float32
        )
        corner[...] += lax.dot_general(
            dense[square:], dense[square:], contract, preferred_element_type=jnp.float32
        )
        return tuple(ranks)

    first = 0
    ranks = (jnp.int32(0),) * n_bas
    for stage, size in enumerate(STAGES):
        if first == EARLY:
            owns[0].wait()
            ranks = lax.fori_loop(
                0, EARLY_TILES // GROUP, functools.partial(gram, late=False), ranks
            )
        for copy in copies[stage * (n_bas - 1) : (stage + 1) * (n_bas - 1)]:
            copy.wait()
        first += size
    owns[1].wait()
    lax.fori_loop(
        EARLY_TILES // GROUP, tiles // GROUP, functools.partial(gram, late=True), ranks
    )
    for a in range(n_aux):
        low, high = a * aux_rows, (a + 1) * aux_rows
        partial[a, :, 0:square] = wide[low:high]
        if low >= square:
            partial[a, :, square:] = corner[low - square : high - square]
    own_rows = aux_rows // n_bas
    turned = wide[square:].T
    for a in range(n_aux):
        low, high = a * aux_rows, min((a + 1) * aux_rows, square)
        if low < square:
            partial[a, 0 : high - low, square:] = turned[low:high]
            if high < low + aux_rows:
                partial[a, high - low :, square:] = corner[0 : low + aux_rows - high]

    core = lax.rem(me, 2)
    n_half = n_aux // 2
    pair = pltpu.make_async_remote_copy(
        src_ref=partial.at[pl.ds((1 - core) * n_half, n_half)],
        dst_ref=pair_in,
        send_sem=pair_send,
        recv_sem=pair_recv,
        device_id={"bas": sibling},
        device_id_type=MESH,
    )
    pair.start()
    pair.wait()
    for i in range(n_half):
        half[i] = partial[core * n_half + i] + pair_in[i]

    keeps = my_aux // n_half == core
    other = jnp.where(keeps, 0, 1)
    copies = []
    for k in range(n_half):
        place = lax.rem(my_aux + k, n_half)
        copies.append(
            pltpu.make_async_remote_copy(
                src_ref=half.at[place],
                dst_ref=partial_in.at[my_aux],
                send_sem=aux_send.at[k],
                recv_sem=aux_recv.at[k + n_half * other],
                device_id={"aux": core * n_half + place},
                device_id_type=MESH,
            )
        )
    for k in range(1, n_half):
        copies[k].start()

    @pl.when(jnp.logical_not(keeps))
    def _():
        copies[0].start()
        for copy in copies:
            copy.wait_send()

    @pl.when(keeps)
    def _():
        partial_in[my_aux] = half[lax.rem(my_aux, n_half)]
        for k in range(1, n_aux):
            pltpu.make_async_remote_copy(
                src_ref=half.at[0],
                dst_ref=partial_in.at[0],
                send_sem=aux_send.at[0],
                recv_sem=aux_recv.at[k],
                device_id={"aux": my_aux},
                device_id_type=MESH,
            ).wait_recv()
        for k in range(1, n_half):
            copies[k].wait_send()
        total = partial_in[0]
        for a in range(1, n_aux):
            total = total + partial_in[a]
        for d in range(n_bas):
            summed[d, 0:own_rows] = total[d * own_rows : (d + 1) * own_rows]
        summed_in[me] = summed[me]

    copies = []
    for k in range(1, n_bas):
        peer = lax.rem(me + k, n_bas)
        copies.append(
            pltpu.make_async_remote_copy(
                src_ref=summed.at[peer],
                dst_ref=summed_in.at[me],
                send_sem=bas_send.at[k],
                recv_sem=bas_recv.at[k],
                device_id={"bas": peer},
                device_id_type=MESH,
            )
        )

    @pl.when(keeps)
    def _():
        for copy in copies:
            copy.start()

    giver = my_aux // n_half
    for k in range(1, n_bas):

        @pl.when(lax.rem(me + n_bas - k, 2) == giver)
        def _(k=k):
            copies[k - 1].wait_recv()

    total = summed_in[giver]
    for d in range(2, n_bas, 2):
        total = total + summed_in[giver + d]
    out_ref[...] = total[0:own_rows]

    @pl.when(keeps)
    def _():
        for copy in copies:
            copy.wait_send()

    for copy in flag_copies:
        copy.wait()
    flagged = flag_in[0]
    for a in range(1, n_aux):
        flagged = jnp.maximum(flagged, flag_in[a])
    flag_out[...] = flagged
    local = pltpu.make_async_copy(flag_out, flag_smem, flag_local)
    local.start()
    local.wait()
    flag_ref[0, 0] = flag_smem[0, 0]


def body(n_aux, n_bas, integrals, coefficients, supports, tile_pattern):
    tiles, blocks = tile_pattern.shape
    window = n_bas * blocks * BAS_TILE
    rows = AUX_TILE // n_bas // 2 * BAS_TILE
    aux_rows = window // n_aux
    own_rows = aux_rows // n_bas
    square = window // 3 * 2
    vmem = pl.BlockSpec(memory_space=pltpu.VMEM)
    dma = pltpu.SemaphoreType.DMA
    bf16, f32, i32 = jnp.bfloat16, jnp.float32, jnp.int32
    result, flag = pl.pallas_call(
        functools.partial(kernel, n_aux, n_bas, tiles, blocks),
        out_shape=(
            jax.ShapeDtypeStruct((own_rows, window), f32),
            jax.ShapeDtypeStruct((1, 1), i32),
        ),
        in_specs=[
            pl.BlockSpec(memory_space=pltpu.SMEM),
            vmem,
            vmem,
            vmem,
            pl.BlockSpec(memory_space=pl.ANY),
        ],
        out_specs=(vmem, pl.BlockSpec(memory_space=pltpu.SMEM)),
        scratch_shapes=[
            pltpu.VMEM((HEAD_TILES, AUX_TILE, blocks, BAS_TILE, SPAN), bf16),
            pltpu.VMEM((tiles, AUX_TILE, blocks, BAS_TILE, SPAN), bf16),
            pltpu.VMEM((2 * ORBITALS, 2 * SPAN), bf16),
            pltpu.VMEM((n_bas, CAP, rows, 2 * ORBITALS), bf16),
            pltpu.VMEM((n_bas, EARLY + 1, rows, 2 * ORBITALS), bf16),
            pltpu.VMEM((n_bas, CAP - EARLY, rows, 2 * ORBITALS), bf16),
            pltpu.VMEM((SPARE, n_bas, rows, 2 * ORBITALS), bf16),
            pltpu.VMEM((SPARE, n_bas, rows, 2 * ORBITALS), bf16),
            pltpu.VMEM((window, GROUP * rows // BAS_TILE * 2 * ORBITALS), bf16),
            pltpu.VMEM((window, square), f32),
            pltpu.VMEM((window - square, window - square), f32),
            pltpu.VMEM((n_aux, aux_rows, window), f32),
            pltpu.VMEM((n_aux // 2, aux_rows, window), f32),
            pltpu.VMEM((n_aux // 2, aux_rows, window), f32),
            pltpu.VMEM((n_aux, aux_rows, window), f32),
            pltpu.VMEM((n_bas, 8, window), f32),
            pltpu.VMEM((n_bas, 8, window), f32),
            pltpu.VMEM((8, 128), i32),
            pltpu.VMEM((n_bas, 8, 128), i32),
            pltpu.SMEM((n_bas, 8, 128), i32),
            pltpu.VMEM((8, 128), i32),
            pltpu.VMEM((n_aux, 8, 128), i32),
            pltpu.SMEM((8, 128), i32),
            pltpu.SMEM((tiles * blocks + 1,), i32),
            pltpu.SMEM((CAP + SPARE,), i32),
            dma,
            dma((tiles,)),
            dma((n_bas,)),
            dma((n_bas,)),
            dma,
            dma((len(STAGES), n_bas)),
            dma((len(STAGES), n_bas)),
            dma((2,)),
            dma,
            dma,
            dma((n_aux,)),
            dma((n_aux,)),
            dma,
            dma,
            dma,
            dma((n_aux,)),
            dma((n_aux,)),
            dma((n_bas,)),
            dma((n_bas,)),
        ],
        compiler_params=pltpu.CompilerParams(
            collective_id=0, has_side_effects=True, vmem_limit_bytes=60 * 2**20
        ),
        name="exchange",
    )(
        tile_pattern.T,
        tile_pattern.T,
        supports.T,
        coefficients.T,
        integrals.reshape(tiles, AUX_TILE, blocks, BAS_TILE, SPAN),
    )
    return lax.cond(
        flag[0, 0] > 0,
        lambda: dense_body(integrals, coefficients, supports, tile_pattern),
        lambda: result,
    )


def solution(mesh):
    in_specs = (P("aux", "bas", None), P(), P(), P("aux", "bas"))
    out_specs = P(("aux", "bas"), None)
    return jax.shard_map(
        functools.partial(body, mesh.shape["aux"], mesh.shape["bas"]),
        mesh=mesh,
        in_specs=in_specs,
        out_specs=out_specs,
        check_vma=False,
    )
```

```python
import functools

import jax
import jax.numpy as jnp
from jax import lax
from jax.experimental import pallas as pl
from jax.experimental.pallas import tpu as pltpu
from jax.sharding import PartitionSpec as P

AUX_TILE = 128
BAS_TILE = 16
ORBITALS = 64
SPAN = 128
MESH = pl.DeviceIdType.MESH

CAP = 31
SPARE = 8
STAGES = (3, 4, 4, 4, 4, 4, 4, 4)
HANDOVER_AFTER = 1
HEAD = 3
HEAD_TILES = 4
EARLY_TILES = 9
EARLY = 27
GROUP = 3


def dense_body(integrals, coefficients, supports, tile_pattern):
    span = integrals.shape[2]
    tile_of = jnp.arange(span) // BAS_TILE
    supported = jnp.any(tile_of[:, None, None] == supports[None, :, :], axis=2)
    orbitals = jnp.where(supported, coefficients, jnp.zeros_like(coefficients))
    screening = jnp.repeat(jnp.repeat(tile_pattern, BAS_TILE, axis=1), AUX_TILE, axis=0).astype(
        jnp.float32
    )
    transformed = jnp.einsum("pmn,ni->pim", integrals, orbitals, preferred_element_type=jnp.float32)
    transformed = (transformed * screening[:, None, :]).astype(jnp.bfloat16)
    contract = (((0,), (0,)), ((), ()))
    redistributed = lax.all_to_all(transformed, "bas", split_axis=1, concat_axis=2, tiled=True)
    window_rows = redistributed.shape[2]
    stacked = redistributed.reshape(-1, window_rows)
    total = lax.dot_general(stacked, stacked, contract, preferred_element_type=jnp.float32)
    for axis in ("aux", "bas"):
        total = total.reshape(lax.axis_size(axis), -1, window_rows)
        total = jnp.sum(lax.all_to_all(total, axis, split_axis=0, concat_axis=0), axis=0)
    return total


def kernel(
    n_aux,
    n_bas,
    tiles,
    blocks,
    pattern_smem,
    pattern_vmem,
    supports_ref,
    coefficients_ref,
    integrals_ref,
    out_ref,
    flag_ref,
    loaded_head,
    loaded,
    weights,
    send_buf,
    recv_early,
    recv_late,
    spare_out,
    spare_in,
    dense,
    wide,
    corner,
    partial,
    pair_in,
    half,
    partial_in,
    summed,
    summed_in,
    pattern_out,
    pattern_in,
    pattern_all,
    flag_out,
    flag_in,
    flag_smem,
    following,
    listed,
    head_sem,
    load_sem,
    pattern_send,
    pattern_recv,
    pattern_local,
    send_sem,
    recv_sem,
    own_sem,
    spare_send,
    spare_recv,
    flag_send,
    flag_recv,
    flag_local,
    pair_send,
    pair_recv,
    aux_send,
    aux_recv,
    bas_send,
    bas_recv,
):
    my_aux = lax.axis_index("aux")
    me = lax.axis_index("bas")
    sibling = me + 1 - 2 * lax.rem(me, 2)
    count = tiles * blocks
    rows = AUX_TILE // n_bas // 2 * BAS_TILE

    head = pltpu.make_async_copy(integrals_ref.at[pl.ds(0, HEAD_TILES)], loaded_head, head_sem)
    head.start()
    loads = []
    for q in range(HEAD_TILES, tiles):
        loads.append(
            pltpu.make_async_copy(integrals_ref.at[q], loaded.at[q], load_sem.at[q])
        )

    barrier = pltpu.get_barrier_semaphore()
    for k in range(1, n_bas):
        pl.semaphore_signal(
            barrier, inc=1, device_id={"bas": lax.rem(me + k, n_bas)}, device_id_type=MESH
        )
    for k in range(1, n_aux):
        pl.semaphore_signal(
            barrier, inc=1, device_id={"aux": lax.rem(my_aux + k, n_aux)}, device_id_type=MESH
        )

    following[count] = jnp.int32(count - 1)
    upcoming = jnp.int32(count - 1)
    for at in reversed(range(count)):
        upcoming = jnp.where(pattern_smem[at % blocks, at // blocks] > 0, at, upcoming)
        following[at] = upcoming
    mine = jnp.int32(0)
    for at in range(count):
        if at == HEAD_TILES * blocks:
            short = mine < HEAD
            mine = jnp.maximum(mine, HEAD)
        mine = mine + pattern_smem[at % blocks, at // blocks]
    at = following[0]
    for s in range(CAP + SPARE):
        if s == HEAD:
            at = jnp.where(short, following[HEAD_TILES * blocks], at)
        listed[s] = at
        at = following[at + 1]

    pattern_out[...] = jnp.zeros_like(pattern_out)
    pattern_out[0:blocks, 0:tiles] = pattern_vmem[...]

    tile_of = lax.broadcasted_iota(jnp.int32, (SPAN, ORBITALS), 0) // BAS_TILE
    named = supports_ref[...]
    supported = tile_of == named[0:1]
    for k in range(1, named.shape[0]):
        supported = supported | (tile_of == named[k : k + 1])
    diagonal = lax.broadcasted_iota(jnp.int32, (ORBITALS, ORBITALS), 0) == (
        lax.broadcasted_iota(jnp.int32, (ORBITALS, ORBITALS), 1)
    )
    turned = lax.dot_general(
        jnp.where(diagonal, 1.0, 0.0).astype(jnp.bfloat16),
        jnp.where(supported, 1.0, 0.0).astype(jnp.bfloat16),
        (((1,), (1,)), ((), ())),
        preferred_element_type=jnp.float32,
    )
    orbitals = jnp.where(turned > 0.5, coefficients_ref[...].astype(jnp.float32), 0.0)
    weights[...] = jnp.zeros_like(weights)
    weights[0:ORBITALS, 0:SPAN] = orbitals.astype(jnp.bfloat16)
    weights[ORBITALS : 2 * ORBITALS, SPAN : 2 * SPAN] = orbitals.astype(jnp.bfloat16)

    head.wait()
    for copy in loads:
        copy.start()
    loads.append(pltpu.make_async_copy(loaded_head, loaded.at[pl.ds(0, HEAD_TILES)], head_sem))
    loads[-1].start()

    def transform(s, share, source, limit):
        at = jnp.minimum(listed[s], limit * blocks - 1)
        tile = at // blocks
        block = at - tile * blocks
        width = AUX_TILE // n_bas
        part = source[tile, pl.ds(share * width, width), block]
        part = part.reshape(width // 2, 2, BAS_TILE, SPAN)
        left = jnp.concatenate(
            [part[:, 0].reshape(rows, SPAN), part[:, 1].reshape(rows, SPAN)], axis=1
        )
        return lax.dot_general(
            left, weights[...], (((1,), (1,)), ((), ())), preferred_element_type=jnp.float32
        ).astype(jnp.bfloat16)

    copies = []
    hand = None
    first = 0
    for stage, size in enumerate(STAGES):
        if first + size > CAP - SPARE and hand is not None:
            hand.wait()
            hand = None

        if first == HEAD:
            for copy in loads:
                copy.wait()
        source, limit = (loaded_head, HEAD_TILES) if first < HEAD else (loaded, tiles)

        def fill(s, carry, mixed=first + size > CAP - SPARE, source=source, limit=limit):
            for share in range(n_bas):
                value = transform(s, share, source, limit)
                if mixed:
                    other = spare_in[CAP - 1 - s, share]
                    value = jnp.where(s < mine, value, other)
                send_buf[share, s] = value
            return carry

        lax.fori_loop(first, first + size, fill, 0)
        if stage == 0:
            pl.semaphore_wait(barrier, n_bas + n_aux - 2)

            pattern_copies = []
            for k in range(1, n_bas):
                pattern_copies.append(
                    pltpu.make_async_remote_copy(
                        src_ref=pattern_out,
                        dst_ref=pattern_in.at[me],
                        send_sem=pattern_send.at[k],
                        recv_sem=pattern_recv.at[k],
                        device_id={"bas": lax.rem(me + k, n_bas)},
                        device_id_type=MESH,
                    )
                )
                pattern_copies[-1].start()
        for k in range(1, n_bas):
            peer = lax.rem(me + k, n_bas)
            where = (recv_early, first) if first < EARLY else (recv_late, first - EARLY)
            copies.append(
                pltpu.make_async_remote_copy(
                    src_ref=send_buf.at[peer, pl.ds(first, size)],
                    dst_ref=where[0].at[me, pl.ds(where[1], size)],
                    send_sem=send_sem.at[stage, k],
                    recv_sem=recv_sem.at[stage, k],
                    device_id={"bas": peer},
                    device_id_type=MESH,
                )
            )
            copies[-1].start()
        if stage == HANDOVER_AFTER:

            def spare(e, carry):
                for share in range(n_bas):
                    spare_out[e, share] = transform(CAP + e, share, loaded, tiles)
                return carry

            lax.fori_loop(0, SPARE, spare, 0)
            hand = pltpu.make_async_remote_copy(
                src_ref=spare_out,
                dst_ref=spare_in,
                send_sem=spare_send,
                recv_sem=spare_recv,
                device_id={"bas": sibling},
                device_id_type=MESH,
            )
            hand.start()
        first += size
    owns = [
        pltpu.make_async_copy(
            send_buf.at[me, pl.ds(0, EARLY)], recv_early.at[me, pl.ds(0, EARLY)], own_sem.at[0]
        ),
        pltpu.make_async_copy(
            send_buf.at[me, pl.ds(EARLY, CAP - EARLY)],
            recv_late.at[me, pl.ds(0, CAP - EARLY)],
            own_sem.at[1],
        ),
    ]
    for copy in owns:
        copy.start()

    recv_early[0, EARLY] = jnp.zeros(recv_early.shape[2:], recv_early.dtype)
    for copy in pattern_copies:
        copy.wait()
    pattern_in[me] = pattern_out[...]
    local = pltpu.make_async_copy(pattern_in, pattern_all, pattern_local)
    local.start()
    local.wait()

    def tally(q, counts):
        return tuple(
            jnp.where(q == HEAD_TILES, jnp.maximum(counts[d], HEAD), counts[d])
            + sum(pattern_all[d, b, q] for b in range(blocks))
            for d in range(n_bas)
        )

    counts = lax.fori_loop(0, tiles, tally, (jnp.int32(0),) * n_bas)
    over = jnp.int32(0)
    for d in range(0, n_bas, 2):
        over = jnp.where(counts[d] + counts[d + 1] > 2 * CAP, 1, over)
    for d in range(n_bas):
        over = jnp.where(counts[d] > CAP + SPARE, 1, over)
    flag_out[...] = jnp.full(flag_out.shape, over, jnp.int32)
    flag_copies = []
    for k in range(1, n_aux):
        flag_copies.append(
            pltpu.make_async_remote_copy(
                src_ref=flag_out,
                dst_ref=flag_in.at[my_aux],
                send_sem=flag_send.at[k],
                recv_sem=flag_recv.at[k],
                device_id={"aux": lax.rem(my_aux + k, n_aux)},
                device_id_type=MESH,
            )
        )
        flag_copies[-1].start()
    flag_in[my_aux] = flag_out[...]

    span_rows = n_bas * blocks * BAS_TILE
    aux_rows = span_rows // n_aux
    square = wide.shape[1]
    depth = rows // BAS_TILE * 128
    wide[...] = jnp.zeros_like(wide)
    corner[...] = jnp.zeros_like(corner)

    def gram(group, ranks, late):
        ranks = list(ranks)
        for step in range(GROUP):
            q = group * GROUP + step
            for d in range(n_bas):
                ranks[d] = jnp.where(q == HEAD_TILES, jnp.maximum(ranks[d], HEAD), ranks[d])
                for b in range(blocks):
                    here = pattern_all[d, b, q] > 0
                    rank = ranks[d]
                    if late:
                        handed = rank >= CAP
                        source = jnp.where(handed, d + 1 - 2 * (d % 2), d)
                        slot = jnp.where(handed, jnp.maximum(2 * CAP - 1 - rank, 0), rank)
                        last = here & (slot >= EARLY)
                        first = here & (slot < EARLY)
                        value = jnp.where(
                            last,
                            recv_late[source, jnp.clip(slot - EARLY, 0, CAP - EARLY - 1)],
                            recv_early[jnp.where(first, source, 0), jnp.where(first, slot, EARLY)],
                        )
                    else:
                        value = recv_early[jnp.where(here, d, 0), jnp.where(here, rank, EARLY)]
                    top = (d * blocks + b) * BAS_TILE
                    for u in range(rows // BAS_TILE):
                        at = step * depth + u * 128
                        dense[top : top + BAS_TILE, at : at + 128] = value[
                            u * BAS_TILE : (u + 1) * BAS_TILE
                        ]
                    ranks[d] = rank + pattern_all[d, b, q]
        contract = (((1,), (1,)), ((), ()))
        wide[...] += lax.dot_general(
            dense[...], dense[0:square], contract, preferred_element_type=jnp.float32
        )
        corner[...] += lax.dot_general(
            dense[square:], dense[square:], contract, preferred_element_type=jnp.float32
        )
        return tuple(ranks)

    first = 0
    ranks = (jnp.int32(0),) * n_bas
    for stage, size in enumerate(STAGES):
        if first == EARLY:
            owns[0].wait()
            ranks = lax.fori_loop(
                0, EARLY_TILES // GROUP, functools.partial(gram, late=False), ranks
            )
        for copy in copies[stage * (n_bas - 1) : (stage + 1) * (n_bas - 1)]:
            copy.wait()
        first += size
    owns[1].wait()
    lax.fori_loop(
        EARLY_TILES // GROUP, tiles // GROUP, functools.partial(gram, late=True), ranks
    )
    for a in range(n_aux):
        low, high = a * aux_rows, (a + 1) * aux_rows
        partial[a, :, 0:square] = wide[low:high]
        if low >= square:
            partial[a, :, square:] = corner[low - square : high - square]
    own_rows = aux_rows // n_bas
    turned = wide[square:].T
    for a in range(n_aux):
        low, high = a * aux_rows, min((a + 1) * aux_rows, square)
        if low < square:
            partial[a, 0 : high - low, square:] = turned[low:high]
            if high < low + aux_rows:
                partial[a, high - low :, square:] = corner[0 : low + aux_rows - high]

    core = lax.rem(me, 2)
    n_half = n_aux // 2
    pair = pltpu.make_async_remote_copy(
        src_ref=partial.at[pl.ds((1 - core) * n_half, n_half)],
        dst_ref=pair_in,
        send_sem=pair_send,
        recv_sem=pair_recv,
        device_id={"bas": sibling},
        device_id_type=MESH,
    )
    pair.start()
    pair.wait()
    for i in range(n_half):
        half[i] = partial[core * n_half + i] + pair_in[i]

    keeps = my_aux // n_half == core
    other = jnp.where(keeps, 0, 1)
    copies = []
    for k in range(n_half):
        place = lax.rem(my_aux + k, n_half)
        copies.append(
            pltpu.make_async_remote_copy(
                src_ref=half.at[place],
                dst_ref=partial_in.at[my_aux],
                send_sem=aux_send.at[k],
                recv_sem=aux_recv.at[k + n_half * other],
                device_id={"aux": core * n_half + place},
                device_id_type=MESH,
            )
        )
    for k in range(1, n_half):
        copies[k].start()

    @pl.when(jnp.logical_not(keeps))
    def _():
        copies[0].start()
        for copy in copies:
            copy.wait_send()

    @pl.when(keeps)
    def _():
        partial_in[my_aux] = half[lax.rem(my_aux, n_half)]
        for k in range(1, n_aux):
            pltpu.make_async_remote_copy(
                src_ref=half.at[0],
                dst_ref=partial_in.at[0],
                send_sem=aux_send.at[0],
                recv_sem=aux_recv.at[k],
                device_id={"aux": my_aux},
                device_id_type=MESH,
            ).wait_recv()
        for k in range(1, n_half):
            copies[k].wait_send()
        total = partial_in[0]
        for a in range(1, n_aux):
            total = total + partial_in[a]
        for d in range(n_bas):
            summed[d, 0:own_rows] = total[d * own_rows : (d + 1) * own_rows]
        summed_in[me] = summed[me]

    copies = []
    for k in range(1, n_bas):
        peer = lax.rem(me + k, n_bas)
        copies.append(
            pltpu.make_async_remote_copy(
                src_ref=summed.at[peer],
                dst_ref=summed_in.at[me],
                send_sem=bas_send.at[k],
                recv_sem=bas_recv.at[k],
                device_id={"bas": peer},
                device_id_type=MESH,
            )
        )

    @pl.when(keeps)
    def _():
        for copy in copies:
            copy.start()

    giver = my_aux // n_half
    for k in range(1, n_bas):

        @pl.when(lax.rem(me + n_bas - k, 2) == giver)
        def _(k=k):
            copies[k - 1].wait_recv()

    total = summed_in[giver]
    for d in range(2, n_bas, 2):
        total = total + summed_in[giver + d]
    out_ref[...] = total[0:own_rows]

    @pl.when(keeps)
    def _():
        for copy in copies:
            copy.wait_send()

    for copy in flag_copies:
        copy.wait()
    flagged = flag_in[0]
    for a in range(1, n_aux):
        flagged = jnp.maximum(flagged, flag_in[a])
    flag_out[...] = flagged
    local = pltpu.make_async_copy(flag_out, flag_smem, flag_local)
    local.start()
    local.wait()
    flag_ref[0, 0] = flag_smem[0, 0]


def body(n_aux, n_bas, integrals, coefficients, supports, tile_pattern):
    tiles, blocks = tile_pattern.shape
    window = n_bas * blocks * BAS_TILE
    rows = AUX_TILE // n_bas // 2 * BAS_TILE
    aux_rows = window // n_aux
    own_rows = aux_rows // n_bas
    square = window // 3 * 2
    vmem = pl.BlockSpec(memory_space=pltpu.VMEM)
    dma = pltpu.SemaphoreType.DMA
    bf16, f32, i32 = jnp.bfloat16, jnp.float32, jnp.int32
    result, flag = pl.pallas_call(
        functools.partial(kernel, n_aux, n_bas, tiles, blocks),
        out_shape=(
            jax.ShapeDtypeStruct((own_rows, window), f32),
            jax.ShapeDtypeStruct((1, 1), i32),
        ),
        in_specs=[
            pl.BlockSpec(memory_space=pltpu.SMEM),
            vmem,
            vmem,
            vmem,
            pl.BlockSpec(memory_space=pl.ANY),
        ],
        out_specs=(vmem, pl.BlockSpec(memory_space=pltpu.SMEM)),
        scratch_shapes=[
            pltpu.VMEM((HEAD_TILES, AUX_TILE, blocks, BAS_TILE, SPAN), bf16),
            pltpu.VMEM((tiles, AUX_TILE, blocks, BAS_TILE, SPAN), bf16),
            pltpu.VMEM((2 * ORBITALS, 2 * SPAN), bf16),
            pltpu.VMEM((n_bas, CAP, rows, 2 * ORBITALS), bf16),
            pltpu.VMEM((n_bas, EARLY + 1, rows, 2 * ORBITALS), bf16),
            pltpu.VMEM((n_bas, CAP - EARLY, rows, 2 * ORBITALS), bf16),
            pltpu.VMEM((SPARE, n_bas, rows, 2 * ORBITALS), bf16),
            pltpu.VMEM((SPARE, n_bas, rows, 2 * ORBITALS), bf16),
            pltpu.VMEM((window, GROUP * rows // BAS_TILE * 2 * ORBITALS), bf16),
            pltpu.VMEM((window, square), f32),
            pltpu.VMEM((window - square, window - square), f32),
            pltpu.VMEM((n_aux, aux_rows, window), f32),
            pltpu.VMEM((n_aux // 2, aux_rows, window), f32),
            pltpu.VMEM((n_aux // 2, aux_rows, window), f32),
            pltpu.VMEM((n_aux, aux_rows, window), f32),
            pltpu.VMEM((n_bas, 8, window), f32),
            pltpu.VMEM((n_bas, 8, window), f32),
            pltpu.VMEM((8, 128), i32),
            pltpu.VMEM((n_bas, 8, 128), i32),
            pltpu.SMEM((n_bas, 8, 128), i32),
            pltpu.VMEM((8, 128), i32),
            pltpu.VMEM((n_aux, 8, 128), i32),
            pltpu.SMEM((8, 128), i32),
            pltpu.SMEM((tiles * blocks + 1,), i32),
            pltpu.SMEM((CAP + SPARE,), i32),
            dma,
            dma((tiles,)),
            dma((n_bas,)),
            dma((n_bas,)),
            dma,
            dma((len(STAGES), n_bas)),
            dma((len(STAGES), n_bas)),
            dma((2,)),
            dma,
            dma,
            dma((n_aux,)),
            dma((n_aux,)),
            dma,
            dma,
            dma,
            dma((n_aux,)),
            dma((n_aux,)),
            dma((n_bas,)),
            dma((n_bas,)),
        ],
        compiler_params=pltpu.CompilerParams(
            collective_id=0, has_side_effects=True, vmem_limit_bytes=60 * 2**20
        ),
        name="exchange",
    )(
        tile_pattern.T,
        tile_pattern.T,
        supports.T,
        coefficients.T,
        integrals.reshape(tiles, AUX_TILE, blocks, BAS_TILE, SPAN),
    )
    return lax.cond(
        flag[0, 0] > 0,
        lambda: dense_body(integrals, coefficients, supports, tile_pattern),
        lambda: result,
    )


def solution(mesh):
    in_specs = (P("aux", "bas", None), P(), P(), P("aux", "bas"))
    out_specs = P(("aux", "bas"), None)
    return jax.shard_map(
        functools.partial(body, mesh.shape["aux"], mesh.shape["bas"]),
        mesh=mesh,
        in_specs=in_specs,
        out_specs=out_specs,
        check_vma=False,
    )
```

```python
import functools

import jax
import jax.numpy as jnp
from jax import lax
from jax.experimental import pallas as pl
from jax.experimental.pallas import tpu as pltpu
from jax.sharding import PartitionSpec as P

AUX_TILE = 128
BAS_TILE = 16
ORBITALS = 64
SPAN = 128
MESH = pl.DeviceIdType.MESH

CAP = 31
SPARE = 8
STAGES = (3, 4, 4, 4, 4, 4, 4, 4)
HANDOVER_AFTER = 1
HEAD = 3
HEAD_TILES = 4
EARLY_TILES = 9
EARLY = 27
GROUP = 3


def dense_body(integrals, coefficients, supports, tile_pattern):
    span = integrals.shape[2]
    tile_of = jnp.arange(span) // BAS_TILE
    supported = jnp.any(tile_of[:, None, None] == supports[None, :, :], axis=2)
    orbitals = jnp.where(supported, coefficients, jnp.zeros_like(coefficients))
    screening = jnp.repeat(jnp.repeat(tile_pattern, BAS_TILE, axis=1), AUX_TILE, axis=0).astype(
        jnp.float32
    )
    transformed = jnp.einsum("pmn,ni->pim", integrals, orbitals, preferred_element_type=jnp.float32)
    transformed = (transformed * screening[:, None, :]).astype(jnp.bfloat16)
    contract = (((0,), (0,)), ((), ()))
    redistributed = lax.all_to_all(transformed, "bas", split_axis=1, concat_axis=2, tiled=True)
    window_rows = redistributed.shape[2]
    stacked = redistributed.reshape(-1, window_rows)
    total = lax.dot_general(stacked, stacked, contract, preferred_element_type=jnp.float32)
    for axis in ("aux", "bas"):
        total = total.reshape(lax.axis_size(axis), -1, window_rows)
        total = jnp.sum(lax.all_to_all(total, axis, split_axis=0, concat_axis=0), axis=0)
    return total


def kernel(
    n_aux,
    n_bas,
    tiles,
    blocks,
    pattern_smem,
    pattern_vmem,
    supports_ref,
    coefficients_ref,
    integrals_ref,
    out_ref,
    flag_ref,
    loaded_head,
    loaded,
    weights,
    send_buf,
    recv_early,
    recv_late,
    spare_out,
    spare_in,
    dense,
    wide,
    corner,
    partial,
    pair_in,
    half,
    partial_in,
    summed,
    summed_in,
    pattern_out,
    pattern_in,
    pattern_all,
    flag_out,
    flag_in,
    flag_smem,
    following,
    listed,
    head_sem,
    load_sem,
    pattern_send,
    pattern_recv,
    pattern_local,
    send_sem,
    recv_sem,
    own_sem,
    spare_send,
    spare_recv,
    flag_send,
    flag_recv,
    flag_local,
    pair_send,
    pair_recv,
    aux_send,
    aux_recv,
    bas_send,
    bas_recv,
):
    my_aux = lax.axis_index("aux")
    me = lax.axis_index("bas")
    sibling = me + 1 - 2 * lax.rem(me, 2)
    count = tiles * blocks
    rows = AUX_TILE // n_bas // 2 * BAS_TILE

    head = pltpu.make_async_copy(integrals_ref.at[pl.ds(0, HEAD_TILES)], loaded_head, head_sem)
    head.start()
    loads = []
    for q in range(HEAD_TILES, tiles):
        loads.append(
            pltpu.make_async_copy(integrals_ref.at[q], loaded.at[q], load_sem.at[q])
        )

    barrier = pltpu.get_barrier_semaphore()
    for k in range(1, n_bas):
        pl.semaphore_signal(
            barrier, inc=1, device_id={"bas": lax.rem(me + k, n_bas)}, device_id_type=MESH
        )
    for k in range(1, n_aux):
        pl.semaphore_signal(
            barrier, inc=1, device_id={"aux": lax.rem(my_aux + k, n_aux)}, device_id_type=MESH
        )

    following[count] = jnp.int32(count - 1)
    upcoming = jnp.int32(count - 1)
    for at in reversed(range(count)):
        upcoming = jnp.where(pattern_smem[at % blocks, at // blocks] > 0, at, upcoming)
        following[at] = upcoming
    mine = jnp.int32(0)
    for at in range(count):
        if at == HEAD_TILES * blocks:
            short = mine < HEAD
            mine = jnp.maximum(mine, HEAD)
        mine = mine + pattern_smem[at % blocks, at // blocks]
    at = following[0]
    for s in range(CAP + SPARE):
        if s == HEAD:
            at = jnp.where(short, following[HEAD_TILES * blocks], at)
        listed[s] = at
        at = following[at + 1]

    pattern_out[...] = jnp.zeros_like(pattern_out)
    pattern_out[0:blocks, 0:tiles] = pattern_vmem[...]

    tile_of = lax.broadcasted_iota(jnp.int32, (SPAN, ORBITALS), 0) // BAS_TILE
    named = supports_ref[...]
    supported = tile_of == named[0:1]
    for k in range(1, named.shape[0]):
        supported = supported | (tile_of == named[k : k + 1])
    diagonal = lax.broadcasted_iota(jnp.int32, (ORBITALS, ORBITALS), 0) == (
        lax.broadcasted_iota(jnp.int32, (ORBITALS, ORBITALS), 1)
    )
    turned = lax.dot_general(
        jnp.where(diagonal, 1.0, 0.0).astype(jnp.bfloat16),
        jnp.where(supported, 1.0, 0.0).astype(jnp.bfloat16),
        (((1,), (1,)), ((), ())),
        preferred_element_type=jnp.float32,
    )
    orbitals = jnp.where(turned > 0.5, coefficients_ref[...].astype(jnp.float32), 0.0)
    weights[...] = jnp.zeros_like(weights)
    weights[0:ORBITALS, 0:SPAN] = orbitals.astype(jnp.bfloat16)
    weights[ORBITALS : 2 * ORBITALS, SPAN : 2 * SPAN] = orbitals.astype(jnp.bfloat16)

    head.wait()
    for copy in loads:
        copy.start()
    loads.append(pltpu.make_async_copy(loaded_head, loaded.at[pl.ds(0, HEAD_TILES)], head_sem))
    loads[-1].start()

    def transform(s, share, source, limit):
        at = jnp.minimum(listed[s], limit * blocks - 1)
        tile = at // blocks
        block = at - tile * blocks
        width = AUX_TILE // n_bas
        part = source[tile, pl.ds(share * width, width), block]
        part = part.reshape(width // 2, 2, BAS_TILE, SPAN)
        left = jnp.concatenate(
            [part[:, 0].reshape(rows, SPAN), part[:, 1].reshape(rows, SPAN)], axis=1
        )
        return lax.dot_general(
            left, weights[...], (((1,), (1,)), ((), ())), preferred_element_type=jnp.float32
        ).astype(jnp.bfloat16)

    copies = []
    hand = None
    first = 0
    for stage, size in enumerate(STAGES):
        if first + size > CAP - SPARE and hand is not None:
            hand.wait()
            hand = None

        if first == HEAD:
            for copy in loads:
                copy.wait()
        source, limit = (loaded_head, HEAD_TILES) if first < HEAD else (loaded, tiles)

        def fill(s, carry, mixed=first + size > CAP - SPARE, source=source, limit=limit):
            for share in range(n_bas):
                value = transform(s, share, source, limit)
                if mixed:
                    other = spare_in[CAP - 1 - s, share]
                    value = jnp.where(s < mine, value, other)
                send_buf[share, s] = value
            return carry

        lax.fori_loop(first, first + size, fill, 0)
        if stage == 0:
            pl.semaphore_wait(barrier, n_bas + n_aux - 2)

            pattern_copies = []
            for k in range(1, n_bas):
                pattern_copies.append(
                    pltpu.make_async_remote_copy(
                        src_ref=pattern_out,
                        dst_ref=pattern_in.at[me],
                        send_sem=pattern_send.at[k],
                        recv_sem=pattern_recv.at[k],
                        device_id={"bas": lax.rem(me + k, n_bas)},
                        device_id_type=MESH,
                    )
                )
                pattern_copies[-1].start()
        for k in range(1, n_bas):
            peer = lax.rem(me + k, n_bas)
            where = (recv_early, first) if first < EARLY else (recv_late, first - EARLY)
            copies.append(
                pltpu.make_async_remote_copy(
                    src_ref=send_buf.at[peer, pl.ds(first, size)],
                    dst_ref=where[0].at[me, pl.ds(where[1], size)],
                    send_sem=send_sem.at[stage, k],
                    recv_sem=recv_sem.at[stage, k],
                    device_id={"bas": peer},
                    device_id_type=MESH,
                )
            )
            copies[-1].start()
        if stage == HANDOVER_AFTER:

            def spare(e, carry):
                for share in range(n_bas):
                    spare_out[e, share] = transform(CAP + e, share, loaded, tiles)
                return carry

            lax.fori_loop(0, SPARE, spare, 0)
            hand = pltpu.make_async_remote_copy(
                src_ref=spare_out,
                dst_ref=spare_in,
                send_sem=spare_send,
                recv_sem=spare_recv,
                device_id={"bas": sibling},
                device_id_type=MESH,
            )
            hand.start()
        first += size
    owns = [
        pltpu.make_async_copy(
            send_buf.at[me, pl.ds(0, EARLY)], recv_early.at[me, pl.ds(0, EARLY)], own_sem.at[0]
        ),
        pltpu.make_async_copy(
            send_buf.at[me, pl.ds(EARLY, CAP - EARLY)],
            recv_late.at[me, pl.ds(0, CAP - EARLY)],
            own_sem.at[1],
        ),
    ]
    for copy in owns:
        copy.start()

    recv_early[0, EARLY] = jnp.zeros(recv_early.shape[2:], recv_early.dtype)
    for copy in pattern_copies:
        copy.wait()
    pattern_in[me] = pattern_out[...]
    local = pltpu.make_async_copy(pattern_in, pattern_all, pattern_local)
    local.start()
    local.wait()

    def tally(q, counts):
        return tuple(
            jnp.where(q == HEAD_TILES, jnp.maximum(counts[d], HEAD), counts[d])
            + sum(pattern_all[d, b, q] for b in range(blocks))
            for d in range(n_bas)
        )

    counts = lax.fori_loop(0, tiles, tally, (jnp.int32(0),) * n_bas)
    over = jnp.int32(0)
    for d in range(0, n_bas, 2):
        over = jnp.where(counts[d] + counts[d + 1] > 2 * CAP, 1, over)
    for d in range(n_bas):
        over = jnp.where(counts[d] > CAP + SPARE, 1, over)
    flag_out[...] = jnp.full(flag_out.shape, over, jnp.int32)
    flag_copies = []
    for k in range(1, n_aux):
        flag_copies.append(
            pltpu.make_async_remote_copy(
                src_ref=flag_out,
                dst_ref=flag_in.at[my_aux],
                send_sem=flag_send.at[k],
                recv_sem=flag_recv.at[k],
                device_id={"aux": lax.rem(my_aux + k, n_aux)},
                device_id_type=MESH,
            )
        )
        flag_copies[-1].start()
    flag_in[my_aux] = flag_out[...]

    span_rows = n_bas * blocks * BAS_TILE
    aux_rows = span_rows // n_aux
    square = wide.shape[1]
    depth = rows // BAS_TILE * 128
    wide[...] = jnp.zeros_like(wide)
    corner[...] = jnp.zeros_like(corner)

    def gram(group, ranks, late):
        ranks = list(ranks)
        for step in range(GROUP):
            q = group * GROUP + step
            for d in range(n_bas):
                ranks[d] = jnp.where(q == HEAD_TILES, jnp.maximum(ranks[d], HEAD), ranks[d])
                for b in range(blocks):
                    here = pattern_all[d, b, q] > 0
                    rank = ranks[d]
                    if late:
                        handed = rank >= CAP
                        source = jnp.where(handed, d + 1 - 2 * (d % 2), d)
                        slot = jnp.where(handed, jnp.maximum(2 * CAP - 1 - rank, 0), rank)
                        last = here & (slot >= EARLY)
                        first = here & (slot < EARLY)
                        value = jnp.where(
                            last,
                            recv_late[source, jnp.clip(slot - EARLY, 0, CAP - EARLY - 1)],
                            recv_early[jnp.where(first, source, 0), jnp.where(first, slot, EARLY)],
                        )
                    else:
                        value = recv_early[jnp.where(here, d, 0), jnp.where(here, rank, EARLY)]
                    top = (d * blocks + b) * BAS_TILE
                    for u in range(rows // BAS_TILE):
                        at = step * depth + u * 128
                        dense[top : top + BAS_TILE, at : at + 128] = value[
                            u * BAS_TILE : (u + 1) * BAS_TILE
                        ]
                    ranks[d] = rank + pattern_all[d, b, q]
        contract = (((1,), (1,)), ((), ()))
        wide[...] += lax.dot_general(
            dense[...], dense[0:square], contract, preferred_element_type=jnp.float32
        )
        corner[...] += lax.dot_general(
            dense[square:], dense[square:], contract, preferred_element_type=jnp.float32
        )
        return tuple(ranks)

    first = 0
    ranks = (jnp.int32(0),) * n_bas
    for stage, size in enumerate(STAGES):
        if first == EARLY:
            owns[0].wait()
            ranks = lax.fori_loop(
                0, EARLY_TILES // GROUP, functools.partial(gram, late=False), ranks
            )
        for copy in copies[stage * (n_bas - 1) : (stage + 1) * (n_bas - 1)]:
            copy.wait()
        first += size
    owns[1].wait()
    lax.fori_loop(
        EARLY_TILES // GROUP, tiles // GROUP, functools.partial(gram, late=True), ranks
    )
    for a in range(n_aux):
        low, high = a * aux_rows, (a + 1) * aux_rows
        partial[a, :, 0:square] = wide[low:high]
        if low >= square:
            partial[a, :, square:] = corner[low - square : high - square]
    own_rows = aux_rows // n_bas
    turned = wide[square:].T
    for a in range(n_aux):
        low, high = a * aux_rows, min((a + 1) * aux_rows, square)
        if low < square:
            partial[a, 0 : high - low, square:] = turned[low:high]
            if high < low + aux_rows:
                partial[a, high - low :, square:] = corner[0 : low + aux_rows - high]

    for copy in flag_copies:
        copy.wait()
    flagged = flag_in[0]
    for a in range(1, n_aux):
        flagged = jnp.maximum(flagged, flag_in[a])

    core = lax.rem(me, 2)
    chip = me // 2
    n_half = n_aux // 2
    n_chip = n_bas // 2
    chip_rows = 2 * own_rows
    pair = pltpu.make_async_remote_copy(
        src_ref=partial.at[pl.ds((1 - core) * n_half, n_half)],
        dst_ref=pair_in,
        send_sem=pair_send,
        recv_sem=pair_recv,
        device_id={"bas": sibling},
        device_id_type=MESH,
    )
    pair.start()
    pair.wait()
    for i in range(n_half):
        both = partial[core * n_half + i] + pair_in[i]
        for c in range(n_chip):
            half[i * n_chip + c, 0:chip_rows] = both[c * chip_rows : (c + 1) * chip_rows]

    keeps = my_aux // n_half == core
    copies = []
    for k in range(n_half):
        place = lax.rem(my_aux + k, n_half)
        for c in range(n_chip):
            column = lax.rem(chip + c, n_chip)
            copies.append(
                pltpu.make_async_remote_copy(
                    src_ref=half.at[place * n_chip + column],
                    dst_ref=partial_in.at[my_aux * n_chip + chip],
                    send_sem=aux_send,
                    recv_sem=aux_recv,
                    device_id={"aux": core * n_half + place, "bas": 2 * column + core},
                    device_id_type=MESH,
                )
            )
    for copy in copies[1:]:
        copy.start()

    def counted(number):
        return pltpu.make_async_remote_copy(
            src_ref=partial_in.at[pl.ds(0, number)],
            dst_ref=partial_in.at[pl.ds(0, number)],
            send_sem=aux_send,
            recv_sem=aux_recv,
            device_id={"bas": sibling},
            device_id_type=MESH,
        )

    last = pltpu.make_async_remote_copy(
        src_ref=summed,
        dst_ref=summed_in,
        send_sem=bas_send,
        recv_sem=bas_recv,
        device_id={"bas": sibling},
        device_id_type=MESH,
    )

    @pl.when(keeps)
    def _():
        partial_in[my_aux * n_chip + chip] = half[lax.rem(my_aux, n_half) * n_chip + chip]
        counted(n_aux * n_chip - 1).wait_recv()
        total = partial_in[0]
        for a in range(1, n_aux * n_chip):
            total = total + partial_in[a]
        upper, lower = total[0:own_rows], total[own_rows:chip_rows]
        summed[0:own_rows] = jnp.where(core == 0, lower, upper)
        last.start()
        out_ref[...] = jnp.where(core == 0, upper, lower)
        counted(n_half * n_chip - 1).wait_send()
        last.wait_send()

    @pl.when(jnp.logical_not(keeps))
    def _():
        copies[0].start()
        counted(n_half * n_chip).wait_send()
        last.wait_recv()
        out_ref[...] = summed_in[0:own_rows]

    flag_out[...] = flagged
    local = pltpu.make_async_copy(flag_out, flag_smem, flag_local)
    local.start()
    local.wait()
    flag_ref[0, 0] = flag_smem[0, 0]


def body(n_aux, n_bas, integrals, coefficients, supports, tile_pattern):
    tiles, blocks = tile_pattern.shape
    window = n_bas * blocks * BAS_TILE
    rows = AUX_TILE // n_bas // 2 * BAS_TILE
    aux_rows = window // n_aux
    own_rows = aux_rows // n_bas
    square = window // 3 * 2
    vmem = pl.BlockSpec(memory_space=pltpu.VMEM)
    dma = pltpu.SemaphoreType.DMA
    bf16, f32, i32 = jnp.bfloat16, jnp.float32, jnp.int32
    result, flag = pl.pallas_call(
        functools.partial(kernel, n_aux, n_bas, tiles, blocks),
        out_shape=(
            jax.ShapeDtypeStruct((own_rows, window), f32),
            jax.ShapeDtypeStruct((1, 1), i32),
        ),
        in_specs=[
            pl.BlockSpec(memory_space=pltpu.SMEM),
            vmem,
            vmem,
            vmem,
            pl.BlockSpec(memory_space=pl.ANY),
        ],
        out_specs=(vmem, pl.BlockSpec(memory_space=pltpu.SMEM)),
        scratch_shapes=[
            pltpu.VMEM((HEAD_TILES, AUX_TILE, blocks, BAS_TILE, SPAN), bf16),
            pltpu.VMEM((tiles, AUX_TILE, blocks, BAS_TILE, SPAN), bf16),
            pltpu.VMEM((2 * ORBITALS, 2 * SPAN), bf16),
            pltpu.VMEM((n_bas, CAP, rows, 2 * ORBITALS), bf16),
            pltpu.VMEM((n_bas, EARLY + 1, rows, 2 * ORBITALS), bf16),
            pltpu.VMEM((n_bas, CAP - EARLY, rows, 2 * ORBITALS), bf16),
            pltpu.VMEM((SPARE, n_bas, rows, 2 * ORBITALS), bf16),
            pltpu.VMEM((SPARE, n_bas, rows, 2 * ORBITALS), bf16),
            pltpu.VMEM((window, GROUP * rows // BAS_TILE * 2 * ORBITALS), bf16),
            pltpu.VMEM((window, square), f32),
            pltpu.VMEM((window - square, window - square), f32),
            pltpu.VMEM((n_aux, aux_rows, window), f32),
            pltpu.VMEM((n_aux // 2, aux_rows, window), f32),
            pltpu.VMEM((n_aux // 2 * n_bas // 2, 8, window), f32),
            pltpu.VMEM((n_aux * n_bas // 2, 8, window), f32),
            pltpu.VMEM((8, window), f32),
            pltpu.VMEM((8, window), f32),
            pltpu.VMEM((8, 128), i32),
            pltpu.VMEM((n_bas, 8, 128), i32),
            pltpu.SMEM((n_bas, 8, 128), i32),
            pltpu.VMEM((8, 128), i32),
            pltpu.VMEM((n_aux, 8, 128), i32),
            pltpu.SMEM((8, 128), i32),
            pltpu.SMEM((tiles * blocks + 1,), i32),
            pltpu.SMEM((CAP + SPARE,), i32),
            dma,
            dma((tiles,)),
            dma((n_bas,)),
            dma((n_bas,)),
            dma,
            dma((len(STAGES), n_bas)),
            dma((len(STAGES), n_bas)),
            dma((2,)),
            dma,
            dma,
            dma((n_aux,)),
            dma((n_aux,)),
            dma,
            dma,
            dma,
            dma,
            dma,
            dma,
            dma,
        ],
        compiler_params=pltpu.CompilerParams(
            collective_id=0, has_side_effects=True, vmem_limit_bytes=60 * 2**20
        ),
        name="exchange",
    )(
        tile_pattern.T,
        tile_pattern.T,
        supports.T,
        coefficients.T,
        integrals.reshape(tiles, AUX_TILE, blocks, BAS_TILE, SPAN),
    )
    return lax.cond(
        flag[0, 0] > 0,
        lambda: dense_body(integrals, coefficients, supports, tile_pattern),
        lambda: result,
    )


def solution(mesh):
    in_specs = (P("aux", "bas", None), P(), P(), P("aux", "bas"))
    out_specs = P(("aux", "bas"), None)
    return jax.shard_map(
        functools.partial(body, mesh.shape["aux"], mesh.shape["bas"]),
        mesh=mesh,
        in_specs=in_specs,
        out_specs=out_specs,
        check_vma=False,
    )
```

```python
import functools
import math

import jax
import jax.numpy as jnp
from jax import lax
from jax.experimental import pallas as pl
from jax.experimental.pallas import tpu as pltpu
from jax.sharding import PartitionSpec as P

AUX_TILE = 128
BAS_TILE = 16
ORBITALS = 64
SPAN = 128
MESH = pl.DeviceIdType.MESH

CAP = 31
SPARE = 8
STAGES = (1, 2, 4, 4, 4, 4, 4, 4, 4)
HANDOVER_AFTER = 3
HEAD = 3
HEAD_TILES = 4
EARLY_TILES = 9
EARLY = 27
GROUP = 3


def dense_body(integrals, coefficients, supports, tile_pattern):
    span = integrals.shape[2]
    tile_of = jnp.arange(span) // BAS_TILE
    supported = jnp.any(tile_of[:, None, None] == supports[None, :, :], axis=2)
    orbitals = jnp.where(supported, coefficients, jnp.zeros_like(coefficients))
    screening = jnp.repeat(jnp.repeat(tile_pattern, BAS_TILE, axis=1), AUX_TILE, axis=0).astype(
        jnp.float32
    )
    transformed = jnp.einsum("pmn,ni->pim", integrals, orbitals, preferred_element_type=jnp.float32)
    transformed = (transformed * screening[:, None, :]).astype(jnp.bfloat16)
    contract = (((0,), (0,)), ((), ()))
    redistributed = lax.all_to_all(transformed, "bas", split_axis=1, concat_axis=2, tiled=True)
    window_rows = redistributed.shape[2]
    stacked = redistributed.reshape(-1, window_rows)
    total = lax.dot_general(stacked, stacked, contract, preferred_element_type=jnp.float32)
    for axis in ("aux", "bas"):
        total = total.reshape(lax.axis_size(axis), -1, window_rows)
        total = jnp.sum(lax.all_to_all(total, axis, split_axis=0, concat_axis=0), axis=0)
    return total


def kernel(
    n_aux,
    n_bas,
    tiles,
    blocks,
    pattern_smem,
    pattern_vmem,
    supports_ref,
    coefficients_ref,
    integrals_ref,
    out_ref,
    flag_ref,
    loaded_head,
    loaded,
    weights,
    send_buf,
    recv_early,
    recv_late,
    spare_out,
    spare_in,
    dense,
    wide,
    corner,
    partial,
    pair_in,
    half,
    partial_in,
    summed,
    summed_in,
    pattern_out,
    pattern_in,
    pattern_all,
    flag_out,
    flag_row,
    flag_mid,
    flag_in,
    flag_smem,
    following,
    listed,
    head_sem,
    load_sem,
    pattern_send,
    pattern_recv,
    pattern_local,
    send_sem,
    recv_sem,
    own_sem,
    spare_send,
    spare_recv,
    flag_send,
    flag_recv,
    flag_local,
    pair_send,
    pair_recv,
    aux_send,
    aux_recv,
    bas_send,
    bas_recv,
):
    my_aux = lax.axis_index("aux")
    me = lax.axis_index("bas")
    sibling = me + 1 - 2 * lax.rem(me, 2)
    count = tiles * blocks
    rows = AUX_TILE // n_bas // 2 * BAS_TILE

    head = pltpu.make_async_copy(integrals_ref.at[pl.ds(0, HEAD_TILES)], loaded_head, head_sem)
    head.start()
    loads = []
    for q in range(HEAD_TILES, tiles):
        loads.append(
            pltpu.make_async_copy(integrals_ref.at[q], loaded.at[q], load_sem.at[q])
        )

    barrier = pltpu.get_barrier_semaphore()
    for k in range(1, n_bas):
        pl.semaphore_signal(
            barrier, inc=1, device_id={"bas": lax.rem(me + k, n_bas)}, device_id_type=MESH
        )
    side = math.isqrt(n_aux)
    across, along = my_aux // side, lax.rem(my_aux, side)
    row_peers = [across * side + lax.rem(along + k, side) for k in range(1, side)]
    column_peers = [lax.rem(across + k, side) * side + along for k in range(1, side)]
    for peer in row_peers + column_peers:
        pl.semaphore_signal(barrier, inc=1, device_id={"aux": peer}, device_id_type=MESH)

    following[count] = jnp.int32(count - 1)
    upcoming = jnp.int32(count - 1)
    for at in reversed(range(count)):
        upcoming = jnp.where(pattern_smem[at % blocks, at // blocks] > 0, at, upcoming)
        following[at] = upcoming
    mine = jnp.int32(0)
    for at in range(count):
        if at == HEAD_TILES * blocks:
            short = mine < HEAD
            mine = jnp.maximum(mine, HEAD)
        mine = mine + pattern_smem[at % blocks, at // blocks]
    at = following[0]
    for s in range(CAP + SPARE):
        if s == HEAD:
            at = jnp.where(short, following[HEAD_TILES * blocks], at)
        listed[s] = at
        at = following[at + 1]

    pattern_out[...] = jnp.zeros_like(pattern_out)
    pattern_out[0:blocks, 0:tiles] = pattern_vmem[...]

    tile_of = lax.broadcasted_iota(jnp.int32, (SPAN, ORBITALS), 0) // BAS_TILE
    named = supports_ref[...]
    supported = tile_of == named[0:1]
    for k in range(1, named.shape[0]):
        supported = supported | (tile_of == named[k : k + 1])
    diagonal = lax.broadcasted_iota(jnp.int32, (ORBITALS, ORBITALS), 0) == (
        lax.broadcasted_iota(jnp.int32, (ORBITALS, ORBITALS), 1)
    )
    turned = lax.dot_general(
        jnp.where(diagonal, 1.0, 0.0).astype(jnp.bfloat16),
        jnp.where(supported, 1.0, 0.0).astype(jnp.bfloat16),
        (((1,), (1,)), ((), ())),
        preferred_element_type=jnp.float32,
    )
    orbitals = jnp.where(turned > 0.5, coefficients_ref[...].astype(jnp.float32), 0.0)
    weights[...] = jnp.zeros_like(weights)
    weights[0:ORBITALS, 0:SPAN] = orbitals.astype(jnp.bfloat16)
    weights[ORBITALS : 2 * ORBITALS, SPAN : 2 * SPAN] = orbitals.astype(jnp.bfloat16)

    head.wait()
    for copy in loads:
        copy.start()
    loads.append(pltpu.make_async_copy(loaded_head, loaded.at[pl.ds(0, HEAD_TILES)], head_sem))
    loads[-1].start()

    def transform(s, share, source, limit):
        at = jnp.minimum(listed[s], limit * blocks - 1)
        tile = at // blocks
        block = at - tile * blocks
        width = AUX_TILE // n_bas
        part = source[tile, pl.ds(share * width, width), block]
        part = part.reshape(width // 2, 2, BAS_TILE, SPAN)
        left = jnp.concatenate(
            [part[:, 0].reshape(rows, SPAN), part[:, 1].reshape(rows, SPAN)], axis=1
        )
        return lax.dot_general(
            left, weights[...], (((1,), (1,)), ((), ())), preferred_element_type=jnp.float32
        ).astype(jnp.bfloat16)

    copies = []
    hand = None
    first = 0
    for stage, size in enumerate(STAGES):
        if first + size > CAP - SPARE and hand is not None:
            hand.wait()
            hand = None

        if first == HEAD:
            for copy in loads:
                copy.wait()
        source, limit = (loaded_head, HEAD_TILES) if first < HEAD else (loaded, tiles)

        def fill(s, carry, mixed=first + size > CAP - SPARE, source=source, limit=limit):
            for share in range(n_bas):
                value = transform(s, share, source, limit)
                if mixed:
                    other = spare_in[CAP - 1 - s, share]
                    value = jnp.where(s < mine, value, other)
                send_buf[share, s] = value
            return carry

        lax.fori_loop(first, first + size, fill, 0)
        if stage == 0:
            pl.semaphore_wait(barrier, n_bas + 2 * side - 3)

            pattern_copies = []
            for k in range(1, n_bas):
                pattern_copies.append(
                    pltpu.make_async_remote_copy(
                        src_ref=pattern_out,
                        dst_ref=pattern_in.at[me],
                        send_sem=pattern_send.at[k],
                        recv_sem=pattern_recv.at[k],
                        device_id={"bas": lax.rem(me + k, n_bas)},
                        device_id_type=MESH,
                    )
                )
                pattern_copies[-1].start()
        for k in sorted(range(1, n_bas), key=lambda k: abs(k - n_bas // 2)):
            peer = lax.rem(me + k, n_bas)
            where = (recv_early, first) if first < EARLY else (recv_late, first - EARLY)
            copies.append(
                pltpu.make_async_remote_copy(
                    src_ref=send_buf.at[peer, pl.ds(first, size)],
                    dst_ref=where[0].at[me, pl.ds(where[1], size)],
                    send_sem=send_sem.at[stage, k],
                    recv_sem=recv_sem.at[stage, k],
                    device_id={"bas": peer},
                    device_id_type=MESH,
                )
            )
            copies[-1].start()
        if stage == HANDOVER_AFTER:

            def spare(e, carry):
                for share in range(n_bas):
                    spare_out[e, share] = transform(CAP + e, share, loaded, tiles)
                return carry

            lax.fori_loop(0, SPARE, spare, 0)
            hand = pltpu.make_async_remote_copy(
                src_ref=spare_out,
                dst_ref=spare_in,
                send_sem=spare_send,
                recv_sem=spare_recv,
                device_id={"bas": sibling},
                device_id_type=MESH,
            )
            hand.start()
        first += size
    owns = [
        pltpu.make_async_copy(
            send_buf.at[me, pl.ds(0, EARLY)], recv_early.at[me, pl.ds(0, EARLY)], own_sem.at[0]
        ),
        pltpu.make_async_copy(
            send_buf.at[me, pl.ds(EARLY, CAP - EARLY)],
            recv_late.at[me, pl.ds(0, CAP - EARLY)],
            own_sem.at[1],
        ),
    ]
    for copy in owns:
        copy.start()

    recv_early[0, EARLY] = jnp.zeros(recv_early.shape[2:], recv_early.dtype)
    for copy in pattern_copies:
        copy.wait()
    pattern_in[me] = pattern_out[...]
    local = pltpu.make_async_copy(pattern_in, pattern_all, pattern_local)
    local.start()
    local.wait()

    def tally(q, counts):
        return tuple(
            jnp.where(q == HEAD_TILES, jnp.maximum(counts[d], HEAD), counts[d])
            + sum(pattern_all[d, b, q] for b in range(blocks))
            for d in range(n_bas)
        )

    counts = lax.fori_loop(0, tiles, tally, (jnp.int32(0),) * n_bas)
    over = jnp.int32(0)
    for d in range(0, n_bas, 2):
        over = jnp.where(counts[d] + counts[d + 1] > 2 * CAP, 1, over)
    for d in range(n_bas):
        over = jnp.where(counts[d] > CAP + SPARE, 1, over)
    flag_out[...] = jnp.full(flag_out.shape, over, jnp.int32)

    def pass_flag(flag, landing, place, peers, lane):
        return [
            pltpu.make_async_remote_copy(
                src_ref=flag,
                dst_ref=landing.at[place],
                send_sem=flag_send.at[lane + k],
                recv_sem=flag_recv.at[lane + k],
                device_id={"aux": peer},
                device_id_type=MESH,
            )
            for k, peer in enumerate(peers)
        ]

    flag_copies = pass_flag(flag_out, flag_row, along, row_peers, 0)
    for copy in flag_copies:
        copy.start()
    flag_row[along] = flag_out[...]

    span_rows = n_bas * blocks * BAS_TILE
    aux_rows = span_rows // n_aux
    square = wide.shape[1]
    depth = rows // BAS_TILE * 128
    wide[...] = jnp.zeros_like(wide)
    corner[...] = jnp.zeros_like(corner)

    def gram(group, ranks, late):
        ranks = list(ranks)
        for step in range(GROUP):
            q = group * GROUP + step
            for d in range(n_bas):
                ranks[d] = jnp.where(q == HEAD_TILES, jnp.maximum(ranks[d], HEAD), ranks[d])
                for b in range(blocks):
                    here = pattern_all[d, b, q] > 0
                    rank = ranks[d]
                    if late:
                        handed = rank >= CAP
                        source = jnp.where(handed, d + 1 - 2 * (d % 2), d)
                        slot = jnp.where(handed, jnp.maximum(2 * CAP - 1 - rank, 0), rank)
                        last = here & (slot >= EARLY)
                        first = here & (slot < EARLY)
                        value = jnp.where(
                            last,
                            recv_late[source, jnp.clip(slot - EARLY, 0, CAP - EARLY - 1)],
                            recv_early[jnp.where(first, source, 0), jnp.where(first, slot, EARLY)],
                        )
                    else:
                        value = recv_early[jnp.where(here, d, 0), jnp.where(here, rank, EARLY)]
                    top = (d * blocks + b) * BAS_TILE
                    for u in range(rows // BAS_TILE):
                        at = step * depth + u * 128
                        dense[top : top + BAS_TILE, at : at + 128] = value[
                            u * BAS_TILE : (u + 1) * BAS_TILE
                        ]
                    ranks[d] = rank + pattern_all[d, b, q]
        contract = (((1,), (1,)), ((), ()))
        wide[...] += lax.dot_general(
            dense[...], dense[0:square], contract, preferred_element_type=jnp.float32
        )
        corner[...] += lax.dot_general(
            dense[square:], dense[square:], contract, preferred_element_type=jnp.float32
        )
        return tuple(ranks)

    first = 0
    ranks = (jnp.int32(0),) * n_bas
    for stage, size in enumerate(STAGES):
        if first == EARLY:
            for copy in flag_copies:
                copy.wait()
            flagged = flag_row[0]
            for a in range(1, side):
                flagged = jnp.maximum(flagged, flag_row[a])
            flag_mid[...] = flagged
            flag_copies = pass_flag(flag_mid, flag_in, across, column_peers, side)
            for copy in flag_copies:
                copy.start()
            flag_in[across] = flag_mid[...]
            owns[0].wait()
            ranks = lax.fori_loop(
                0, EARLY_TILES // GROUP, functools.partial(gram, late=False), ranks
            )
        for copy in copies[stage * (n_bas - 1) : (stage + 1) * (n_bas - 1)]:
            copy.wait()
        first += size
    owns[1].wait()
    lax.fori_loop(
        EARLY_TILES // GROUP, tiles // GROUP, functools.partial(gram, late=True), ranks
    )
    for a in range(n_aux):
        low, high = a * aux_rows, (a + 1) * aux_rows
        partial[a, :, 0:square] = wide[low:high]
        if low >= square:
            partial[a, :, square:] = corner[low - square : high - square]
    own_rows = aux_rows // n_bas
    turned = wide[square:].T
    for a in range(n_aux):
        low, high = a * aux_rows, min((a + 1) * aux_rows, square)
        if low < square:
            partial[a, 0 : high - low, square:] = turned[low:high]
            if high < low + aux_rows:
                partial[a, high - low :, square:] = corner[0 : low + aux_rows - high]

    for copy in flag_copies:
        copy.wait()
    flagged = flag_in[0]
    for a in range(1, side):
        flagged = jnp.maximum(flagged, flag_in[a])

    core = lax.rem(me, 2)
    chip = me // 2
    n_half = n_aux // 2
    n_chip = n_bas // 2
    chip_rows = 2 * own_rows
    pair = pltpu.make_async_remote_copy(
        src_ref=partial.at[pl.ds((1 - core) * n_half, n_half)],
        dst_ref=pair_in,
        send_sem=pair_send,
        recv_sem=pair_recv,
        device_id={"bas": sibling},
        device_id_type=MESH,
    )
    pair.start()
    pair.wait()
    for i in range(n_half):
        both = partial[core * n_half + i] + pair_in[i]
        for c in range(n_chip):
            half[i * n_chip + c, 0:chip_rows] = both[c * chip_rows : (c + 1) * chip_rows]

    keeps = my_aux // n_half == core
    copies = []
    for k in range(n_half):
        place = lax.rem(my_aux + k, n_half)
        for c in range(n_chip):
            column = lax.rem(chip + c, n_chip)
            copies.append(
                pltpu.make_async_remote_copy(
                    src_ref=half.at[place * n_chip + column],
                    dst_ref=partial_in.at[my_aux * n_chip + chip],
                    send_sem=aux_send,
                    recv_sem=aux_recv,
                    device_id={"aux": core * n_half + place, "bas": 2 * column + core},
                    device_id_type=MESH,
                )
            )
    for copy in copies[1:]:
        copy.start()

    def counted(number):
        return pltpu.make_async_remote_copy(
            src_ref=partial_in.at[pl.ds(0, number)],
            dst_ref=partial_in.at[pl.ds(0, number)],
            send_sem=aux_send,
            recv_sem=aux_recv,
            device_id={"bas": sibling},
            device_id_type=MESH,
        )

    last = pltpu.make_async_remote_copy(
        src_ref=summed,
        dst_ref=summed_in,
        send_sem=bas_send,
        recv_sem=bas_recv,
        device_id={"bas": sibling},
        device_id_type=MESH,
    )

    @pl.when(keeps)
    def _():
        partial_in[my_aux * n_chip + chip] = half[lax.rem(my_aux, n_half) * n_chip + chip]
        counted(n_aux * n_chip - 1).wait_recv()
        total = partial_in[0]
        for a in range(1, n_aux * n_chip):
            total = total + partial_in[a]
        upper, lower = total[0:own_rows], total[own_rows:chip_rows]
        summed[0:own_rows] = jnp.where(core == 0, lower, upper)
        last.start()
        out_ref[...] = jnp.where(core == 0, upper, lower)
        counted(n_half * n_chip - 1).wait_send()
        last.wait_send()

    @pl.when(jnp.logical_not(keeps))
    def _():
        copies[0].start()
        counted(n_half * n_chip).wait_send()
        last.wait_recv()
        out_ref[...] = summed_in[0:own_rows]

    flag_out[...] = flagged
    local = pltpu.make_async_copy(flag_out, flag_smem, flag_local)
    local.start()
    local.wait()
    flag_ref[0, 0] = flag_smem[0, 0]


def body(n_aux, n_bas, integrals, coefficients, supports, tile_pattern):
    tiles, blocks = tile_pattern.shape
    window = n_bas * blocks * BAS_TILE
    rows = AUX_TILE // n_bas // 2 * BAS_TILE
    aux_rows = window // n_aux
    own_rows = aux_rows // n_bas
    square = window // 3 * 2
    side = math.isqrt(n_aux)
    vmem = pl.BlockSpec(memory_space=pltpu.VMEM)
    dma = pltpu.SemaphoreType.DMA
    bf16, f32, i32 = jnp.bfloat16, jnp.float32, jnp.int32
    result, flag = pl.pallas_call(
        functools.partial(kernel, n_aux, n_bas, tiles, blocks),
        out_shape=(
            jax.ShapeDtypeStruct((own_rows, window), f32),
            jax.ShapeDtypeStruct((1, 1), i32),
        ),
        in_specs=[
            pl.BlockSpec(memory_space=pltpu.SMEM),
            vmem,
            vmem,
            vmem,
            pl.BlockSpec(memory_space=pl.ANY),
        ],
        out_specs=(vmem, pl.BlockSpec(memory_space=pltpu.SMEM)),
        scratch_shapes=[
            pltpu.VMEM((HEAD_TILES, AUX_TILE, blocks, BAS_TILE, SPAN), bf16),
            pltpu.VMEM((tiles, AUX_TILE, blocks, BAS_TILE, SPAN), bf16),
            pltpu.VMEM((2 * ORBITALS, 2 * SPAN), bf16),
            pltpu.VMEM((n_bas, CAP, rows, 2 * ORBITALS), bf16),
            pltpu.VMEM((n_bas, EARLY + 1, rows, 2 * ORBITALS), bf16),
            pltpu.VMEM((n_bas, CAP - EARLY, rows, 2 * ORBITALS), bf16),
            pltpu.VMEM((SPARE, n_bas, rows, 2 * ORBITALS), bf16),
            pltpu.VMEM((SPARE, n_bas, rows, 2 * ORBITALS), bf16),
            pltpu.VMEM((window, GROUP * rows // BAS_TILE * 2 * ORBITALS), bf16),
            pltpu.VMEM((window, square), f32),
            pltpu.VMEM((window - square, window - square), f32),
            pltpu.VMEM((n_aux, aux_rows, window), f32),
            pltpu.VMEM((n_aux // 2, aux_rows, window), f32),
            pltpu.VMEM((n_aux // 2 * n_bas // 2, 8, window), f32),
            pltpu.VMEM((n_aux * n_bas // 2, 8, window), f32),
            pltpu.VMEM((8, window), f32),
            pltpu.VMEM((8, window), f32),
            pltpu.VMEM((8, 128), i32),
            pltpu.VMEM((n_bas, 8, 128), i32),
            pltpu.SMEM((n_bas, 8, 128), i32),
            pltpu.VMEM((8, 128), i32),
            pltpu.VMEM((side, 8, 128), i32),
            pltpu.VMEM((8, 128), i32),
            pltpu.VMEM((side, 8, 128), i32),
            pltpu.SMEM((8, 128), i32),
            pltpu.SMEM((tiles * blocks + 1,), i32),
            pltpu.SMEM((CAP + SPARE,), i32),
            dma,
            dma((tiles,)),
            dma((n_bas,)),
            dma((n_bas,)),
            dma,
            dma((len(STAGES), n_bas)),
            dma((len(STAGES), n_bas)),
            dma((2,)),
            dma,
            dma,
            dma((2 * side,)),
            dma((2 * side,)),
            dma,
            dma,
            dma,
            dma,
            dma,
            dma,
            dma,
        ],
        compiler_params=pltpu.CompilerParams(
            collective_id=0, has_side_effects=True, vmem_limit_bytes=60 * 2**20
        ),
        name="exchange",
    )(
        tile_pattern.T,
        tile_pattern.T,
        supports.T,
        coefficients.T,
        integrals.reshape(tiles, AUX_TILE, blocks, BAS_TILE, SPAN),
    )
    return lax.cond(
        flag[0, 0] > 0,
        lambda: dense_body(integrals, coefficients, supports, tile_pattern),
        lambda: result,
    )


def solution(mesh):
    in_specs = (P("aux", "bas", None), P(), P(), P("aux", "bas"))
    out_specs = P(("aux", "bas"), None)
    return jax.shard_map(
        functools.partial(body, mesh.shape["aux"], mesh.shape["bas"]),
        mesh=mesh,
        in_specs=in_specs,
        out_specs=out_specs,
        check_vma=False,
    )
```
